32 devices in a mesh: groups: 2 (over y), chan: 4 (over z), rows: 2 (over x), cols: 2 (over core).
Axes of the slice: x: 2, y: 2, z: 4, core: 2. Of those that a mesh axis runs over, the one named last changes fastest.
Arguments:
- image: bfloat16 [1536, 16, 256], P('chan', ('groups', 'rows'), 'cols'), parts along dimension 1, may hold values from -40 to 40
- kernel: float32 [1536, 49], P('chan'), may hold values from -0.875 to 0.875
- layer_norm_weight: float32 [1536], P('chan'), may hold values from 0.1 to 1.9
- w_expand: bfloat16 [6144, 1536], P('chan'), may hold values from -0.21875 to 0.21875
- bias_expand: float32 [6144], P('chan'), may hold values from -3 to 3
- w_reduce: bfloat16 [1536, 6144], P(None, 'chan'), may hold values from -0.109375 to 0.109375
- layer_scale: float32 [1536], P('chan'), may hold values from 0.5 to 2
- cotangent: bfloat16 [1536, 16, 256], P('chan', ('groups', 'rows'), 'cols'), parts along dimension 1, may hold values from -6 to 6
Outputs:
- output: bfloat16 [1536, 16, 256], P('chan', ('groups', 'rows'), 'cols'), parts along dimension 1
- grad_input: bfloat16 [1536, 16, 256], P('chan', ('groups', 'rows'), 'cols'), parts along dimension 1
- grad_expand: bfloat16 [12288, 1536], P(('groups', 'chan')), parts along dimension 0
- grad_reduce: bfloat16 [3072, 6144], P('groups', 'chan'), parts along dimension 0
- grad_kernel: float32 [3072, 49], P(('groups', 'chan')), parts along dimension 0
The draws below stay inside these ranges and needn't reach their ends.
There are 2 independent parts, one for each index of `groups`. The reference program is written for one: setup_inputs(seed, part) draws one part's arguments, and reference() takes and returns one part's arrays. A program takes and returns all parts, laid end to end along the dimension named above; an argument that names none is the same for every part. Nothing has to cross between parts.
All inputs are finite; a program needn't handle non-finite values.
Results may differ from the reference program's by a relative error of at most 0.015.
Values may be sent and summed in bfloat16 or wider, within the bound.
No kernel may reach another device: no remote copies, remote signals or barrier semaphores. Data moves between devices by JAX's collectives and lax.ppermute only.
A program may use at most 128 MiB of HBM per device.

```python
import math
import jax
import jax.numpy as jnp
from jax import lax

CHANNEL_COUNT = 1536
HID = 6144
KS = 7
H_DEV = 4
W_DEV = 128
HEIGHT = 8
WIDTH = 256
N_CHAN = 4
N_ROWS = 2
N_COLS = 2


def draw_image(key, part):
    base_key = jax.random.fold_in(key, 11)
    noise_key, jitter_key = jax.random.split(base_key, 2)
    noise = jnp.clip(jax.random.normal(noise_key, (CHANNEL_COUNT, HEIGHT, WIDTH), jnp.float32), -4.0, 4.0)
    position = jnp.arange(CHANNEL_COUNT, dtype=jnp.float32) / CHANNEL_COUNT
    jitter = jax.random.uniform(jitter_key, (CHANNEL_COUNT,), jnp.float32, -0.1, 0.1)
    channel_scale = 0.3 * jnp.power(10.0, position + jitter)
    values = channel_scale[:, None, None] * noise
    return values.astype(jnp.bfloat16)


def raised(entries, key, source, target, shards_of, factor):
    owner, partner = [(jnp.arange(entries.shape[dim]) // (entries.shape[dim] // shards_of)).reshape([-1 if axis == dim else 1 for axis in range(entries.ndim)]) for dim in (source, target)]
    chosen = jax.random.permutation(key, shards_of)[partner]
    strong = (owner == chosen) | (owner == (partner + shards_of // 2) % shards_of)
    return jnp.where(strong, factor * entries, entries)


def level_of(own_key, extent, cuts, least, high):
    def one(axis_at, parts):
        steps = jax.random.uniform(jax.random.fold_in(jax.random.fold_in(own_key, 6), axis_at), (parts,), jnp.float32, least / len(cuts), high / len(cuts))
        return jnp.repeat(jnp.exp(steps), extent[axis_at] // parts).reshape((-1,) + (1,) * (len(extent) - axis_at - 1))

    level = one(*cuts[0])
    for cut in cuts[1:]:
        level = level * one(*cut)
    return level


def scatter_about(rng, shape, scale, reach, pieces=(), kind=jnp.bfloat16):
    array = scale * jax.random.normal(rng, shape, jnp.float32)
    if pieces:
        array = array * level_of(rng, shape, pieces, -0.22, 0.18)
    return jnp.clip(array, -reach, reach).astype(kind)


def bell_draw_with(key, shape, spread, reach, pieces, heavy, held_as=jnp.bfloat16):
    result = spread * jax.random.normal(key, shape, jnp.float32)
    if pieces:
        result = result * level_of(key, shape, pieces, -0.22, 0.18)
    return jnp.clip(raised(result, jax.random.fold_in(key, 3), *heavy), -reach, reach).astype(held_as)


def setup_inputs(seed: int = 0, part: int = 0) -> dict:
    key_of = jax.random.split(jax.random.key(seed), 9)
    own_keys = jax.random.split(jax.random.fold_in(key_of[8], part), 9)
    image = draw_image(jax.random.fold_in(jax.random.fold_in(key_of[8], part), 71), part)
    kernel = scatter_about(key_of[1], (CHANNEL_COUNT, KS * KS), (KS * KS) ** -0.5, 0.875, ((0, 4),), jnp.float32)
    layer_norm_weight = jnp.clip(1.0 + 0.18 * jax.random.normal(key_of[2], (CHANNEL_COUNT,), jnp.float32), 0.1, 1.9)
    w_expand = bell_draw_with(key_of[3], (HID, CHANNEL_COUNT), CHANNEL_COUNT ** -0.5, 0.21875, ((0, 4),), (0, 1, 4, 2.0))
    bias_expand = scatter_about(key_of[4], (HID,), 0.5, 3.0, ((0, 4),), jnp.float32)
    w_reduce = bell_draw_with(key_of[5], (CHANNEL_COUNT, HID), HID ** -0.5, 0.109375, ((1, 4),), (1, 0, 4, 2.0))
    layer_scale = jnp.clip(jnp.exp(math.log(2.0) - 1.3862944 * jax.random.uniform(key_of[6], (CHANNEL_COUNT,), jnp.float32) ** level_of(key_of[6], (CHANNEL_COUNT,), ((0, 4),), -0.2, 0.2)), 0.5, 2.0)
    cotangent = scatter_about(own_keys[7], (CHANNEL_COUNT, HEIGHT, WIDTH), 1.0, 6.0, ((0, 4), (1, 2), (2, 2)))
    return dict(image=image, kernel=kernel, layer_norm_weight=layer_norm_weight, w_expand=w_expand, bias_expand=bias_expand, w_reduce=w_reduce, layer_scale=layer_scale, cotangent=cotangent)


epsilon = 1e-06

def gelu_exact(values):
    return 0.5 * values * (1.0 + lax.erf(values * 0.7071067811865476))

def gelu_slope(values):
    return 0.5 * (1.0 + lax.erf(values * 0.7071067811865476)) + values * jnp.exp(-0.5 * values * values) * 0.3989422804014327

def round_back(values):
    return lax.optimization_barrier(values.astype(jnp.bfloat16)).astype(jnp.float32)

def to_tiles(matrix):
    leading = matrix.shape[0]
    shaped = matrix.reshape(leading, N_ROWS, H_DEV, N_COLS, W_DEV)
    shaped = jnp.transpose(shaped, (1, 3, 0, 2, 4))
    return shaped.reshape(N_ROWS * N_COLS, leading, H_DEV * W_DEV)

def reference(image, kernel, layer_norm_weight, w_expand, bias_expand, w_reduce, layer_scale, cotangent):
    half_side = KS // 2
    pixel_count = HEIGHT * WIDTH
    hid_block = HID // N_CHAN
    tile_count = N_ROWS * N_COLS
    padded = jnp.pad(image.astype(jnp.float32), ((0, 0), (half_side, half_side), (half_side, half_side)))
    conv = jnp.zeros((CHANNEL_COUNT, HEIGHT, WIDTH), jnp.float32)
    for tap_row in range(KS):
        for tap_col in range(KS):
            weight = kernel[:, tap_row * KS + tap_col][:, None, None]
            conv = conv + weight * padded[:, tap_row:tap_row + HEIGHT, tap_col:tap_col + WIDTH]
    mean_map = lax.optimization_barrier(jnp.sum(conv, axis=0)) / CHANNEL_COUNT
    mean_removed = conv - mean_map
    var_map = lax.optimization_barrier(jnp.sum(mean_removed * mean_removed, axis=0)) / CHANNEL_COUNT
    inverse_deviation = lax.rsqrt(var_map + epsilon)
    normalized_input = mean_removed * inverse_deviation
    norm_output = (normalized_input * layer_norm_weight[:, None, None]).astype(jnp.bfloat16).reshape(CHANNEL_COUNT, pixel_count)
    pre_act = jnp.dot(w_expand, norm_output, preferred_element_type=jnp.float32) + bias_expand[:, None]
    hidden = gelu_exact(pre_act).astype(jnp.bfloat16)

    def reduce_block(index, summed):
        first = (index * hid_block).astype(jnp.int32)
        weight_block = lax.dynamic_slice_in_dim(w_reduce, first, hid_block, 1)
        act_block = lax.dynamic_slice_in_dim(hidden, first, hid_block, 0)
        return summed + round_back(jnp.dot(weight_block, act_block, preferred_element_type=jnp.float32))
    reduced = lax.fori_loop(0, N_CHAN, reduce_block, jnp.zeros((CHANNEL_COUNT, pixel_count), jnp.float32))
    image_flat = image.reshape(CHANNEL_COUNT, pixel_count).astype(jnp.float32)
    output = (image_flat + layer_scale[:, None] * reduced).astype(jnp.bfloat16).reshape(CHANNEL_COUNT, HEIGHT, WIDTH)
    scaled_cot = (layer_scale[:, None] * cotangent.reshape(CHANNEL_COUNT, pixel_count).astype(jnp.float32)).astype(jnp.bfloat16)
    grad_hidden = jnp.dot(w_reduce.T, scaled_cot, preferred_element_type=jnp.float32)
    grad_pre = (grad_hidden * gelu_slope(pre_act)).astype(jnp.bfloat16)
    cot_tiles = to_tiles(scaled_cot)
    hidden_tiles = to_tiles(hidden)
    pre_tiles = to_tiles(grad_pre)
    normed_tiles = to_tiles(norm_output)

    def weight_tile(index, sums):
        reduce_sum, expand_sum = sums
        cot_tile = lax.dynamic_index_in_dim(cot_tiles, index, 0, keepdims=False)
        hid_tile = lax.dynamic_index_in_dim(hidden_tiles, index, 0, keepdims=False)
        pre_tile = lax.dynamic_index_in_dim(pre_tiles, index, 0, keepdims=False)
        norm_tile = lax.dynamic_index_in_dim(normed_tiles, index, 0, keepdims=False)
        reduce_sum = reduce_sum + round_back(jnp.dot(cot_tile, hid_tile.T, preferred_element_type=jnp.float32))
        expand_sum = expand_sum + round_back(jnp.dot(pre_tile, norm_tile.T, preferred_element_type=jnp.float32))
        return (reduce_sum, expand_sum)
    grad_reduce, grad_expand = lax.fori_loop(0, tile_count, weight_tile, (jnp.zeros((CHANNEL_COUNT, HID), jnp.float32), jnp.zeros((HID, CHANNEL_COUNT), jnp.float32)))

    def normed_block(index, summed):
        first = (index * hid_block).astype(jnp.int32)
        weight_block = lax.dynamic_slice_in_dim(w_expand, first, hid_block, 0)
        pre_block = lax.dynamic_slice_in_dim(grad_pre, first, hid_block, 0)
        return summed + round_back(jnp.dot(weight_block.T, pre_block, preferred_element_type=jnp.float32))
    grad_normed = lax.fori_loop(0, N_CHAN, normed_block, jnp.zeros((CHANNEL_COUNT, pixel_count), jnp.float32)).reshape(CHANNEL_COUNT, HEIGHT, WIDTH)
    normalized_gradient = grad_normed * layer_norm_weight[:, None, None]
    first_average = lax.optimization_barrier(jnp.sum(normalized_gradient, axis=0)) / CHANNEL_COUNT
    cross_average = lax.optimization_barrier(jnp.sum(normalized_gradient * normalized_input, axis=0)) / CHANNEL_COUNT
    convolution_gradient = (normalized_gradient - first_average - normalized_input * cross_average) * inverse_deviation
    grad_padded = jnp.pad(convolution_gradient, ((0, 0), (half_side, half_side), (half_side, half_side)))
    back_conv = jnp.zeros((CHANNEL_COUNT, HEIGHT, WIDTH), jnp.float32)
    kernel_terms = []
    for tap_row in range(KS):
        for tap_col in range(KS):
            weight = kernel[:, tap_row * KS + tap_col][:, None, None]
            back_conv = back_conv + weight * grad_padded[:, 2 * half_side - tap_row:2 * half_side - tap_row + HEIGHT, 2 * half_side - tap_col:2 * half_side - tap_col + WIDTH]
            product = convolution_gradient * padded[:, tap_row:tap_row + HEIGHT, tap_col:tap_col + WIDTH]
            per_tile = lax.optimization_barrier(jnp.sum(product.reshape(CHANNEL_COUNT, N_ROWS, H_DEV, N_COLS, W_DEV), axis=(2, 4)))
            kernel_terms.append(lax.optimization_barrier(jnp.sum(round_back(per_tile), axis=(1, 2))))
    grad_kernel = jnp.stack(kernel_terms, axis=1)
    grad_input = (cotangent.astype(jnp.float32) + back_conv).astype(jnp.bfloat16)
    return (output, grad_input, grad_expand.astype(jnp.bfloat16), grad_reduce.astype(jnp.bfloat16), grad_kernel)
```

```python
import functools

import jax
import jax.numpy as jnp
from jax import lax
from jax.experimental import pallas as pl
from jax.experimental.pallas import tpu as pltpu
from jax.sharding import PartitionSpec as P

KS = 7
HALF = KS // 2
PAD = 16
EPSILON = 1e-06
MIB = 1024 * 1024
F32 = jnp.float32
BF16 = jnp.bfloat16

whole = pl.BlockSpec(memory_space=pltpu.VMEM)


def params(mib):
    return pltpu.CompilerParams(vmem_limit_bytes=mib * MIB)


def shape(dims, dtype):
    return jax.ShapeDtypeStruct(dims, dtype)


def pieces(values):
    high = values.astype(BF16)
    rest = values - high.astype(F32)
    middle = rest.astype(BF16)
    low = (rest - middle.astype(F32)).astype(BF16)
    return high, middle, low


def stacked_rows(values):
    width = values.shape[1]
    row = lax.broadcasted_iota(jnp.int32, (PAD, width), 0)
    block = jnp.zeros((PAD, width), F32)
    for index, part in enumerate(pieces(values)):
        block = jnp.where(row == index, part.astype(F32), block)
    return block.astype(BF16)


def from_sides(low_source, high_source, axis):
    count = lax.axis_size(axis)
    if count == 2:
        index = lax.axis_index(axis)
        sent = jnp.where(index == 0, low_source, high_source)
        got = lax.ppermute(sent, axis, [(0, 1), (1, 0)])
        return got, got
    forward = [(i, i + 1) for i in range(count - 1)]
    backward = [(i + 1, i) for i in range(count - 1)]
    return lax.ppermute(low_source, axis, forward), lax.ppermute(high_source, axis, backward)


def edges(block, axis):
    count = lax.axis_size(axis)
    if count == 2:
        return lax.ppermute(block, axis, [(0, 1), (1, 0)])
    low, high = from_sides(block, block, axis)
    width = block.shape[-1]
    lane = lax.broadcasted_iota(jnp.int32, block.shape, block.ndim - 1)
    return jnp.where(lane < width // 2, high, low)


def surroundings(block):
    rows = block.shape[0]
    above, below = from_sides(block[rows - HALF :], block[:HALF], "rows")
    side = edges(block, "cols")
    if lax.axis_size("rows") == 2:
        corner = edges(above, "cols")
        return block, above, below, side, corner, corner
    return block, above, below, side, edges(above, "cols"), edges(below, "cols")


def border_flags(width):
    row, col = lax.axis_index("rows"), lax.axis_index("cols")
    one = lambda test: jnp.where(test, 1.0, 0.0).astype(F32)
    has_above = one(row > 0)
    has_below = one(row < lax.axis_size("rows") - 1)
    lane = lax.broadcasted_iota(jnp.int32, (1, width), 1)
    seam = jnp.where(lane < width // 2, one(col < lax.axis_size("cols") - 1), one(col > 0))
    return has_above, has_below, seam


def window_rows(refs, flags, at, count):
    block, above, below, side, above_side, below_side = refs
    has_above, has_below, seam = flags
    rows = block.shape[0]
    cut = pl.ds(at, count)
    found = []
    for k in range(HALF):
        found.append((above[k, cut].astype(F32) * has_above, above_side[k, cut].astype(F32) * (has_above * seam)))
    for k in range(rows):
        found.append((block[k, cut].astype(F32), side[k, cut].astype(F32) * seam))
    for k in range(HALF):
        found.append((below[k, cut].astype(F32) * has_below, below_side[k, cut].astype(F32) * (has_below * seam)))
    return found


def moved(pair, offset, lane):
    own, edge = pair
    width = own.shape[1]
    if offset == 0:
        return own
    if offset > 0:
        return pltpu.roll(jnp.where(lane < offset, edge, own), width - offset, 1)
    return pltpu.roll(jnp.where(lane >= width + offset, edge, own), -offset, 1)


def convolve(refs, flags, taps, at, count, flipped):
    rows = refs[0].shape[0]
    width = refs[0].shape[2]
    found = window_rows(refs, flags, at, count)
    lane = lax.broadcasted_iota(jnp.int32, (count, width), 1)
    sums = [None] * rows
    for tap_col in range(KS):
        shifted = [moved(pair, tap_col - HALF, lane) for pair in found]
        for tap_row in range(KS):
            tap = tap_row * KS + tap_col
            tap = KS * KS - 1 - tap if flipped else tap
            weight = jnp.broadcast_to(taps[:, tap : tap + 1], (count, width))
            for k in range(rows):
                term = weight * shifted[k + tap_row]
                sums[k] = term if sums[k] is None else sums[k] + term
    return sums


def forward_conv_kernel(block, above, below, side, above_side, below_side, kernel, packed, centered, local):
    refs = (block, above, below, side, above_side, below_side)
    rows, channels, width = block.shape
    flags = border_flags(width)

    def step(index, totals):
        at = pl.multiple_of(index * PAD, PAD)
        sums = convolve(refs, flags, kernel[pl.ds(at, PAD), :], at, PAD, False)
        for k in range(rows):
            centered[pl.ds(at, PAD), k * width : (k + 1) * width] = sums[k]
        return tuple(total + value[:8] + value[8:] for total, value in zip(totals, sums))

    totals = lax.fori_loop(
        0, channels // PAD, step, tuple(jnp.zeros((8, width), F32) for _ in range(rows))
    )
    mean = jnp.concatenate([jnp.sum(total, axis=0, keepdims=True) for total in totals], axis=1) / channels
    local[...] = jnp.broadcast_to(mean, local.shape)

    def finish(index, carry):
        at = pl.multiple_of(index * PAD, PAD)
        value = centered[pl.ds(at, PAD), :] - mean
        centered[pl.ds(at, PAD), :] = value
        packed[pl.ds(at, PAD), :] = value.astype(BF16)
        return carry

    lax.fori_loop(0, channels // PAD, finish, 0)
    packed[channels:, :] = stacked_rows(mean)


def forward_conv(around, kernel):
    rows, channels, width = around[0].shape
    pixels = rows * width
    return pl.pallas_call(
        forward_conv_kernel,
        out_shape=(
            shape((channels + PAD, pixels), BF16),
            shape((channels, pixels), F32),
            shape((8, pixels), F32),
        ),
        in_specs=[whole] * 7,
        out_specs=(whole,) * 3,
        compiler_params=params(32),
        cost_estimate=pl.CostEstimate(flops=20_000_000, bytes_accessed=4_000_000, transcendentals=0),
        name="conv_forward",
    )(*around, kernel)


def backward_conv_kernel(block, above, below, side, above_side, below_side, kernel, cotangent, result):
    refs = (block, above, below, side, above_side, below_side)
    rows, channels, width = block.shape
    flags = border_flags(width)

    def step(index, carry):
        at = pl.multiple_of(index * PAD, PAD)
        sums = convolve(refs, flags, kernel[pl.ds(at, PAD), :], at, PAD, True)
        for k in range(rows):
            result[k, pl.ds(at, PAD)] = (sums[k] + cotangent[k, pl.ds(at, PAD)].astype(F32)).astype(BF16)
        return carry

    lax.fori_loop(0, channels // PAD, step, 0)


def backward_conv(around, kernel, cotangent):
    return pl.pallas_call(
        backward_conv_kernel,
        out_shape=shape(cotangent.shape, BF16),
        in_specs=[whole] * 8,
        out_specs=whole,
        compiler_params=params(32),
        cost_estimate=pl.CostEstimate(flops=20_000_000, bytes_accessed=4_000_000, transcendentals=0),
        name="conv_backward",
    )(*around, kernel, cotangent)


def kernel_gradient_kernel(block, above, below, side, above_side, below_side, gradient, result):
    refs = (block, above, below, side, above_side, below_side)
    rows, channels, width = block.shape
    flags = border_flags(width)

    def step(index, carry):
        at = pl.multiple_of(index * PAD, PAD)
        found = window_rows(refs, flags, at, PAD)
        lane = lax.broadcasted_iota(jnp.int32, (PAD, width), 1)
        grads = [gradient[k, pl.ds(at, PAD)].astype(F32) for k in range(rows)]
        sums = jnp.zeros((PAD, width), F32)
        for tap_col in range(KS):
            shifted = [moved(pair, tap_col - HALF, lane) for pair in found]
            for tap_row in range(KS):
                total = grads[0] * shifted[tap_row]
                for k in range(1, rows):
                    total = total + grads[k] * shifted[k + tap_row]
                tap = tap_row * KS + tap_col
                sums = jnp.where(lane == tap, jnp.sum(total, axis=1, keepdims=True), sums)
        result[pl.ds(at, PAD), :] = sums
        return carry

    lax.fori_loop(0, channels // PAD, step, 0)


def kernel_gradient(around, gradient):
    rows, channels, width = gradient.shape
    return pl.pallas_call(
        kernel_gradient_kernel,
        out_shape=shape((channels, width), F32),
        in_specs=[whole] * 7,
        out_specs=whole,
        compiler_params=params(32),
        cost_estimate=pl.CostEstimate(flops=20_000_000, bytes_accessed=4_000_000, transcendentals=0),
        name="kernel_gradient",
    )(*around, gradient)


def pack_kernel(cotangent, scale, gain, packed):
    rows, channels, width = cotangent.shape
    for k in range(rows):
        packed[:channels, k * width : (k + 1) * width] = (
            cotangent[k].astype(F32) * scale[...]
        ).astype(BF16)
    packed[channels:, :] = jnp.zeros((PAD, rows * width), BF16)
    packed[channels:, :channels] = stacked_rows(gain[...])


def pack_cotangent(cotangent, scale, gain):
    rows, channels, width = cotangent.shape
    return pl.pallas_call(
        pack_kernel,
        out_shape=shape((channels + PAD, rows * width), BF16),
        in_specs=[whole] * 3,
        out_specs=whole,
        compiler_params=params(32),
        name="pack_cotangent",
    )(cotangent, scale, gain)


def gelu_parts(values):
    cdf = 0.5 * (1.0 + lax.erf(values * 0.7071067811865476))
    slope = cdf + values * jnp.exp(-0.5 * values * values) * 0.3989422804014327
    return values * cdf, slope


ROWS_BY_COLS = (((1,), (0,)), ((), ()))
COLS_BY_COLS = (((0,), (0,)), ((), ()))
ROWS_BY_ROWS = (((1,), (1,)), ((), ()))


def dot(left, right, dims):
    return lax.dot_general(left, right, dims, preferred_element_type=F32)


def unpack_matrix(gathered, target, channels):
    for k in range(gathered.shape[0]):
        target[k * channels : (k + 1) * channels, :] = gathered[k, :channels, :]


def block_kernel(
    steps, conv_all, cot_all, gain, w_expand, bias, w_reduce,
    normed, hidden, grad_pre, reduced, grad_normed, stats, moments,
    cot, reduce_sum, normed_sum,
):
    count = conv_all.shape[0]
    channels = conv_all.shape[1] - PAD
    every = count * channels
    at = pl.program_id(0)

    @pl.when(at == 0)
    def _():
        means = [
            jnp.sum(conv_all[k, channels:, :].astype(F32), axis=0, keepdims=True) for k in range(count)
        ]
        mean = means[0]
        for k in range(1, count):
            mean = mean + means[k]
        mean = mean / count
        squares = jnp.zeros_like(mean)
        for k in range(count):
            value = conv_all[k, :channels, :].astype(F32) + (means[k] - mean)
            squares = squares + jnp.sum(value * value, axis=0, keepdims=True)
        deviation = lax.rsqrt(squares / every + EPSILON)
        for k in range(count):
            value = conv_all[k, :channels, :].astype(F32) + (means[k] - mean)
            cut = slice(k * channels, (k + 1) * channels)
            normed[cut, :] = (value * deviation * gain[cut, :]).astype(BF16)
        row = lax.broadcasted_iota(jnp.int32, stats.shape, 0)
        stats[...] = jnp.where(row == 0, mean, jnp.where(row == 1, deviation, 0.0))
        unpack_matrix(cot_all, cot, channels)
        reduce_sum[...] = jnp.zeros_like(reduce_sum)
        normed_sum[...] = jnp.zeros_like(normed_sum)

    pre = dot(w_expand[...], normed[...], ROWS_BY_COLS) + bias[...]
    active, slope = gelu_parts(pre)
    active = active.astype(BF16)
    hidden[...] = active
    back = dot(w_reduce[...], cot[...], COLS_BY_COLS)
    back = (back * slope).astype(BF16)
    grad_pre[...] = back
    normed_sum[...] += dot(w_expand[...], back, COLS_BY_COLS)
    reduce_sum[...] += dot(w_reduce[...], active, ROWS_BY_COLS)

    @pl.when(at == steps - 1)
    def _():
        reduced[...] = reduce_sum[...].astype(BF16)
        total = normed_sum[...]
        grad_normed[...] = total.astype(BF16)
        first = jnp.sum(total * gain[...], axis=0, keepdims=True)
        cross = jnp.sum(total * normed[...].astype(F32), axis=0, keepdims=True)
        row = lax.broadcasted_iota(jnp.int32, moments.shape, 0)
        moments[...] = jnp.where(row == 0, first, jnp.where(row == 1, cross, 0.0))


def tile_of(hidden_units):
    for size in (256, 128):
        if hidden_units % size == 0:
            return size
    return hidden_units


def fixed(dims):
    return pl.BlockSpec(dims, lambda t: (0,) * len(dims))


def block_forward(conv_all, cot_all, gain, w_expand, bias, w_reduce):
    count, padded, pixels = conv_all.shape
    every = gain.shape[0]
    units = w_expand.shape[0]
    tile = tile_of(units)
    steps = units // tile
    return pl.pallas_call(
        functools.partial(block_kernel, steps),
        grid=(steps,),
        out_shape=(
            shape((every, pixels), BF16),
            shape((units, pixels), BF16),
            shape((units, pixels), BF16),
            shape((every, pixels), BF16),
            shape((every, pixels), BF16),
            shape((8, pixels), F32),
            shape((8, pixels), F32),
        ),
        in_specs=[
            fixed(conv_all.shape),
            fixed(cot_all.shape),
            fixed(gain.shape),
            pl.BlockSpec((tile, every), lambda t: (t, 0)),
            pl.BlockSpec((tile, 1), lambda t: (t, 0)),
            pl.BlockSpec((every, tile), lambda t: (0, t)),
        ],
        out_specs=(
            fixed((every, pixels)),
            pl.BlockSpec((tile, pixels), lambda t: (t, 0)),
            pl.BlockSpec((tile, pixels), lambda t: (t, 0)),
            fixed((every, pixels)),
            fixed((every, pixels)),
            fixed((8, pixels)),
            fixed((8, pixels)),
        ),
        scratch_shapes=[
            pltpu.VMEM((every, pixels), BF16),
            pltpu.VMEM((every, pixels), F32),
            pltpu.VMEM((every, pixels), F32),
        ],
        compiler_params=params(48),
        cost_estimate=pl.CostEstimate(
            flops=8 * units * every * pixels, bytes_accessed=18_000_000, transcendentals=0
        ),
        name="pointwise_block",
    )(conv_all, cot_all, gain, w_expand, bias, w_reduce)


def weight_kernel(
    channels, normed_own, normed_other, cot_own, cot_other, hidden_own, pre_own,
    w_expand, bias, w_reduce, grad_reduce, grad_expand, normed, cot, hidden, grad_pre,
):
    pixels = normed_own.shape[1]
    index = lax.axis_index("rows")
    own = pl.ds(pl.multiple_of(index * pixels, pixels), pixels)
    other = pl.ds(pl.multiple_of((1 - index) * pixels, pixels), pixels)

    @pl.when(pl.program_id(0) == 0)
    def _():
        normed[:, own] = normed_own[...]
        normed[:, other] = normed_other[...]
        for k in range(cot_own.shape[0]):
            cut = slice(k * channels, (k + 1) * channels)
            cot[cut, own] = cot_own[k, :channels, :]
            cot[cut, other] = cot_other[k, :channels, :]

    pre = dot(w_expand[...], normed_other[...], ROWS_BY_COLS) + bias[...]
    active, slope = gelu_parts(pre)
    hidden[:, own] = hidden_own[...]
    hidden[:, other] = active.astype(BF16)
    back = dot(w_reduce[...], cot[:, other], COLS_BY_COLS)
    grad_pre[:, own] = pre_own[...]
    grad_pre[:, other] = (back * slope).astype(BF16)
    grad_reduce[...] = dot(cot[...], hidden[...], ROWS_BY_ROWS).astype(BF16)
    grad_expand[...] = dot(grad_pre[...], normed[...], ROWS_BY_ROWS).astype(BF16)


def weight_gradients(part, parts, normed_own, normed_other, cot_own, cot_other, hidden, grad_pre, w_expand, bias, w_reduce):
    every, pixels = normed_own.shape
    units = w_expand.shape[0]
    tile = tile_of(units)
    steps = units // tile // parts
    first = part * steps
    return pl.pallas_call(
        functools.partial(weight_kernel, cot_own.shape[1] - PAD),
        grid=(steps,),
        out_shape=(shape((every, steps * tile), BF16), shape((steps * tile, every), BF16)),
        in_specs=[
            fixed(normed_own.shape),
            fixed(normed_other.shape),
            fixed(cot_own.shape),
            fixed(cot_other.shape),
            pl.BlockSpec((tile, pixels), lambda t: (t + first, 0)),
            pl.BlockSpec((tile, pixels), lambda t: (t + first, 0)),
            pl.BlockSpec((tile, every), lambda t: (t + first, 0)),
            pl.BlockSpec((tile, 1), lambda t: (t + first, 0)),
            pl.BlockSpec((every, tile), lambda t: (0, t + first)),
        ],
        out_specs=(
            pl.BlockSpec((every, tile), lambda t: (0, t)),
            pl.BlockSpec((tile, every), lambda t: (t, 0)),
        ),
        scratch_shapes=[
            pltpu.VMEM((every, 2 * pixels), BF16),
            pltpu.VMEM((every, 2 * pixels), BF16),
            pltpu.VMEM((tile, 2 * pixels), BF16),
            pltpu.VMEM((tile, 2 * pixels), BF16),
        ],
        compiler_params=params(48),
        cost_estimate=pl.CostEstimate(
            flops=12 * steps * tile * every * pixels, bytes_accessed=18_000_000, transcendentals=0
        ),
        name="weight_gradients",
    )(normed_own, normed_other, cot_own, cot_other, hidden, grad_pre, w_expand, bias, w_reduce)


def norm_gradient_kernel(every, grad_normed, centered, local, stats, moments, gain, result):
    rows, channels, width = result.shape
    mean, deviation = stats[0:1, :], stats[1:2, :]
    first, cross = moments[0:1, :] / every, moments[1:2, :] / every
    shift = local[0:1, :] - mean

    def step(index, carry):
        at = pl.multiple_of(index * PAD, PAD)
        cut = pl.ds(at, PAD)
        hat = (centered[cut, :] + shift) * deviation
        value = grad_normed[cut, :].astype(F32) * gain[cut, :]
        value = ((value - first - hat * cross) * deviation).astype(BF16)
        for k in range(rows):
            result[k, cut] = value[:, k * width : (k + 1) * width]
        return carry

    lax.fori_loop(0, channels // PAD, step, 0)


def norm_gradient(every, dims, grad_normed, centered, local, stats, moments, gain):
    return pl.pallas_call(
        functools.partial(norm_gradient_kernel, every),
        out_shape=shape(dims, BF16),
        in_specs=[whole] * 6,
        out_specs=whole,
        compiler_params=params(32),
        name="norm_gradient",
    )(grad_normed, centered, local, stats, moments, gain)


def swap(values, axis):
    return lax.ppermute(values, axis, [(0, 1), (1, 0)])


def on_device(
    image, kernel, layer_norm_weight, w_expand, bias_expand, w_reduce, layer_scale, cotangent
):
    channels, tile_rows, tile_cols = image.shape
    pixels = tile_rows * tile_cols
    every = w_reduce.shape[0]
    two_tiles = lax.axis_size("rows") == 2 and lax.axis_size("cols") == 2

    cot_rows = jnp.transpose(cotangent, (1, 0, 2))
    packed_cot = pack_cotangent(cot_rows, layer_scale[:, None], layer_norm_weight[None, :])
    cot_all = lax.all_gather(packed_cot, "chan")
    gain_rows = cot_all[:, channels : channels + 3, :channels].astype(F32)
    gain_all = jnp.sum(gain_rows, axis=1).reshape(every, 1)

    image_rows = jnp.transpose(image, (1, 0, 2))
    around = surroundings(image_rows)
    packed_conv, centered, local = forward_conv(around, kernel)
    conv_all = lax.all_gather(packed_conv, "chan")

    bias = bias_expand[:, None]
    normed, hidden, grad_pre, reduced, grad_normed, stats, moments = block_forward(
        conv_all, cot_all, gain_all, w_expand, bias, w_reduce
    )
    grad_normed = lax.psum_scatter(grad_normed, "chan", scatter_dimension=0, tiled=True)
    moments = lax.psum(moments, "chan")
    reduced = lax.psum_scatter(reduced, "chan", scatter_dimension=0, tiled=True)

    if two_tiles:
        cot_other = swap(cot_all, "rows")
        normed_other = swap(normed, "rows")
        parts = 2
        reduce_parts, expand_parts = [], []
        for part in range(parts):
            of_reduce, of_expand = weight_gradients(
                part, parts, normed, normed_other, cot_all, cot_other, hidden, grad_pre,
                w_expand, bias, w_reduce,
            )
            reduce_parts.append(of_reduce.astype(F32) + swap(of_reduce, "cols").astype(F32))
            expand_parts.append(of_expand.astype(F32) + swap(of_expand, "cols").astype(F32))
        grad_reduce = jnp.concatenate(reduce_parts, axis=1).astype(BF16)
        grad_expand = jnp.concatenate(expand_parts, axis=0).astype(BF16)
    else:
        cot_full = cot_all[:, :channels, :].reshape(every, pixels)
        grad_reduce = dot(cot_full, hidden, ROWS_BY_ROWS).astype(BF16)
        grad_expand = dot(grad_pre, normed, ROWS_BY_ROWS).astype(BF16)
        grad_reduce, grad_expand = lax.psum((grad_reduce, grad_expand), ("rows", "cols"))

    gradient = norm_gradient(
        every, image_rows.shape, grad_normed, centered, local, stats, moments,
        layer_norm_weight[:, None],
    )
    grad_around = surroundings(gradient)
    taps = kernel_gradient(around, gradient)[:, : KS * KS]
    if two_tiles:
        taps = taps + swap(taps, "cols")
        taps = taps + swap(taps, "rows")
    else:
        taps = lax.psum(taps, ("rows", "cols"))
    grad_input = jnp.transpose(backward_conv(grad_around, kernel, cot_rows), (1, 0, 2))

    output = (
        image.reshape(channels, pixels).astype(F32)
        + layer_scale[:, None] * reduced.astype(F32)
    ).astype(BF16).reshape(image.shape)
    return output, grad_input, grad_expand, grad_reduce, taps


def solution(mesh):
    placed = (
        P("chan", ("groups", "rows"), "cols"),
        P("chan", None),
        P("chan"),
        P("chan", None),
        P("chan"),
        P(None, "chan"),
        P("chan"),
        P("chan", ("groups", "rows"), "cols"),
    )
    return jax.shard_map(
        on_device,
        mesh=mesh,
        in_specs=placed,
        out_specs=(
            P("chan", ("groups", "rows"), "cols"),
            P("chan", ("groups", "rows"), "cols"),
            P(("groups", "chan"), None),
            P("groups", "chan"),
            P(("groups", "chan"), None),
        ),
        check_vma=False,
    )
```

```python
import functools

import jax
import jax.numpy as jnp
from jax import lax
from jax.experimental import pallas as pl
from jax.experimental.pallas import tpu as pltpu
from jax.sharding import PartitionSpec as P

KS = 7
HALF = KS // 2
PAD = 16
EPSILON = 1e-06
MIB = 1024 * 1024
F32 = jnp.float32
BF16 = jnp.bfloat16

whole = pl.BlockSpec(memory_space=pltpu.VMEM)
anywhere = pl.BlockSpec(memory_space=pl.ANY)
LIGHT = pl.CostEstimate(flops=1000, bytes_accessed=1000, transcendentals=0)


def params(mib):
    return pltpu.CompilerParams(vmem_limit_bytes=mib * MIB)


def shape(dims, dtype):
    return jax.ShapeDtypeStruct(dims, dtype)


def pieces(values):
    high = values.astype(BF16)
    rest = values - high.astype(F32)
    middle = rest.astype(BF16)
    low = (rest - middle.astype(F32)).astype(BF16)
    return high, middle, low


def stacked_rows(*rows):
    width = rows[0].shape[1]
    row = lax.broadcasted_iota(jnp.int32, (PAD, width), 0)
    block = jnp.zeros((PAD, width), F32)
    for first, values in enumerate(rows):
        for index, part in enumerate(pieces(values)):
            block = jnp.where(row == 3 * first + index, part.astype(F32), block)
    return block.astype(BF16)


def unstacked(block, first):
    return jnp.sum(block[3 * first : 3 * first + 3, :].astype(F32), axis=0, keepdims=True)


def from_sides(low_source, high_source, axis):
    count = lax.axis_size(axis)
    if count == 2:
        index = lax.axis_index(axis)
        sent = jnp.where(index == 0, low_source, high_source)
        got = lax.ppermute(sent, axis, [(0, 1), (1, 0)])
        return got, got
    forward = [(i, i + 1) for i in range(count - 1)]
    backward = [(i + 1, i) for i in range(count - 1)]
    return lax.ppermute(low_source, axis, forward), lax.ppermute(high_source, axis, backward)


def edges(block, axis):
    count = lax.axis_size(axis)
    if count == 2:
        return lax.ppermute(block, axis, [(0, 1), (1, 0)])
    low, high = from_sides(block, block, axis)
    width = block.shape[-1]
    lane = lax.broadcasted_iota(jnp.int32, block.shape, block.ndim - 1)
    return jnp.where(lane < width // 2, high, low)


def surroundings(block):
    rows = block.shape[0]
    above, below = from_sides(block[rows - HALF :], block[:HALF], "rows")
    side = edges(block, "cols")
    if lax.axis_size("rows") == 2:
        corner = edges(above, "cols")
        return block, above, below, side, corner, corner
    return block, above, below, side, edges(above, "cols"), edges(below, "cols")


def flag(test):
    return jnp.where(test, 1.0, 0.0).astype(F32)


def fill_shifts(shifts):
    width = shifts.shape[0] // 2
    col = lax.axis_index("cols")
    has_right, has_left = flag(col < lax.axis_size("cols") - 1), flag(col > 0)
    source = lax.broadcasted_iota(jnp.int32, (width, width), 0)
    target = lax.broadcasted_iota(jnp.int32, (width, width), 1)
    for tap in range(KS):
        cut = slice(tap * width, (tap + 1) * width)
        wanted = target + (tap - HALF)
        shifts[:width, cut] = jnp.where(source == wanted, 1.0, 0.0).astype(BF16)
        right = jnp.where(source + width == wanted, has_right, 0.0)
        left = jnp.where(source - width == wanted, has_left, 0.0)
        shifts[width:, cut] = (right + left).astype(BF16)


def shifted_rows(refs, shifts, at, count):
    block, above, below, side, above_side, below_side = refs
    row = lax.axis_index("rows")
    has_above = flag(row > 0).astype(BF16)
    has_below = flag(row < lax.axis_size("rows") - 1).astype(BF16)
    rows = block.shape[0]
    cut = pl.ds(at, count)
    found = [jnp.concatenate([above[k, cut], above_side[k, cut]], axis=1) * has_above for k in range(HALF)]
    found += [jnp.concatenate([block[k, cut], side[k, cut]], axis=1) for k in range(rows)]
    found += [jnp.concatenate([below[k, cut], below_side[k, cut]], axis=1) * has_below for k in range(HALF)]
    return dot(jnp.concatenate(found, axis=0), shifts[...], ROWS_BY_COLS)


def convolve(refs, shifts, taps, at, count, flipped):
    rows, _, width = refs[0].shape
    moved = shifted_rows(refs, shifts, at, count)
    sums = [None] * rows
    for tap_col in range(KS):
        near = [
            moved[k * count : (k + 1) * count, tap_col * width : (tap_col + 1) * width]
            for k in range(rows + KS - 1)
        ]
        for tap_row in range(KS):
            tap = tap_row * KS + tap_col
            tap = KS * KS - 1 - tap if flipped else tap
            weight = jnp.broadcast_to(taps[:, tap : tap + 1], (count, width))
            for k in range(rows):
                term = weight * near[k + tap_row]
                sums[k] = term if sums[k] is None else sums[k] + term
    return sums


def forward_conv_kernel(block, above, below, side, above_side, below_side, kernel, packed, centered, local, shifts):
    refs = (block, above, below, side, above_side, below_side)
    rows, channels, width = block.shape
    fill_shifts(shifts)

    def step(index, totals):
        at = pl.multiple_of(index * PAD, PAD)
        sums = convolve(refs, shifts, kernel[pl.ds(at, PAD), :], at, PAD, False)
        for k in range(rows):
            centered[pl.ds(at, PAD), k * width : (k + 1) * width] = sums[k]
        return tuple(total + value[:8] + value[8:] for total, value in zip(totals, sums))

    totals = lax.fori_loop(
        0, channels // PAD, step, tuple(jnp.zeros((8, width), F32) for _ in range(rows)), unroll=2
    )
    mean = jnp.concatenate([jnp.sum(total, axis=0, keepdims=True) for total in totals], axis=1) / channels
    local[...] = jnp.broadcast_to(mean, local.shape)

    def finish(index, carry):
        at = pl.multiple_of(index * PAD, PAD)
        value = centered[pl.ds(at, PAD), :] - mean
        centered[pl.ds(at, PAD), :] = value
        packed[pl.ds(at, PAD), :] = value.astype(BF16)
        return carry

    lax.fori_loop(0, channels // PAD, finish, 0, unroll=2)
    packed[channels:, :] = stacked_rows(mean)


def shift_scratch(width):
    return [pltpu.VMEM((2 * width, KS * width), BF16)]


def forward_conv(around, kernel):
    rows, channels, width = around[0].shape
    pixels = rows * width
    return pl.pallas_call(
        forward_conv_kernel,
        out_shape=(
            shape((channels + PAD, pixels), BF16),
            shape((channels, pixels), F32),
            shape((8, pixels), F32),
        ),
        in_specs=[whole] * 7,
        out_specs=(whole,) * 3,
        scratch_shapes=shift_scratch(width),
        compiler_params=params(32),
        cost_estimate=LIGHT,
        name="conv_forward",
    )(*around, kernel)


def backward_conv_kernel(block, above, below, side, above_side, below_side, kernel, cotangent, result, shifts):
    refs = (block, above, below, side, above_side, below_side)
    rows, channels, width = block.shape
    fill_shifts(shifts)

    def step(index, carry):
        at = pl.multiple_of(index * PAD, PAD)
        sums = convolve(refs, shifts, kernel[pl.ds(at, PAD), :], at, PAD, True)
        for k in range(rows):
            result[k, pl.ds(at, PAD)] = (sums[k] + cotangent[k, pl.ds(at, PAD)].astype(F32)).astype(BF16)
        return carry

    lax.fori_loop(0, channels // PAD, step, 0, unroll=2)


def backward_conv(around, kernel, cotangent):
    return pl.pallas_call(
        backward_conv_kernel,
        out_shape=shape(cotangent.shape, BF16),
        in_specs=[whole] * 8,
        out_specs=whole,
        scratch_shapes=shift_scratch(cotangent.shape[2]),
        compiler_params=params(32),
        cost_estimate=LIGHT,
        name="conv_backward",
    )(*around, kernel, cotangent)


def kernel_gradient_kernel(block, above, below, side, above_side, below_side, gradient, result, shifts):
    refs = (block, above, below, side, above_side, below_side)
    rows, channels, width = block.shape
    fill_shifts(shifts)

    def step(index, carry):
        at = pl.multiple_of(index * PAD, PAD)
        moved = shifted_rows(refs, shifts, at, PAD)
        lane = lax.broadcasted_iota(jnp.int32, (PAD, width), 1)
        grads = [gradient[k, pl.ds(at, PAD)].astype(F32) for k in range(rows)]
        sums = jnp.zeros((PAD, width), F32)
        for tap_col in range(KS):
            near = [
                moved[k * PAD : (k + 1) * PAD, tap_col * width : (tap_col + 1) * width]
                for k in range(rows + KS - 1)
            ]
            for tap_row in range(KS):
                total = grads[0] * near[tap_row]
                for k in range(1, rows):
                    total = total + grads[k] * near[k + tap_row]
                tap = tap_row * KS + tap_col
                sums = jnp.where(lane == tap, jnp.sum(total, axis=1, keepdims=True), sums)
        result[pl.ds(at, PAD), :] = sums
        return carry

    lax.fori_loop(0, channels // PAD, step, 0, unroll=2)


def kernel_gradient(around, gradient):
    rows, channels, width = gradient.shape
    return pl.pallas_call(
        kernel_gradient_kernel,
        out_shape=shape((channels, width), F32),
        in_specs=[whole] * 7,
        out_specs=whole,
        scratch_shapes=shift_scratch(width),
        compiler_params=params(32),
        cost_estimate=LIGHT,
        name="kernel_gradient",
    )(*around, gradient)


def pack_kernel(cotangent, scale, gain, packed):
    rows, channels, width = cotangent.shape
    for k in range(rows):
        packed[:channels, k * width : (k + 1) * width] = (
            cotangent[k].astype(F32) * scale[...]
        ).astype(BF16)
    packed[channels:, :] = jnp.zeros((PAD, rows * width), BF16)
    packed[channels:, :channels] = stacked_rows(gain[...])


def pack_cotangent(cotangent, scale, gain):
    rows, channels, width = cotangent.shape
    return pl.pallas_call(
        pack_kernel,
        out_shape=shape((channels + PAD, rows * width), BF16),
        in_specs=[whole] * 3,
        out_specs=whole,
        compiler_params=params(32),
        name="pack_cotangent",
    )(cotangent, scale, gain)


def gelu_parts(values):
    cdf = 0.5 * (1.0 + lax.erf(values * 0.7071067811865476))
    slope = cdf + values * jnp.exp(-0.5 * values * values) * 0.3989422804014327
    return values * cdf, slope


ROWS_BY_COLS = (((1,), (0,)), ((), ()))
COLS_BY_COLS = (((0,), (0,)), ((), ()))
ROWS_BY_ROWS = (((1,), (1,)), ((), ()))


def dot(left, right, dims):
    return lax.dot_general(left, right, dims, preferred_element_type=F32)


def tile_of(hidden_units):
    for size in (256, 128):
        if hidden_units % size == 0:
            return size
    return hidden_units


def fixed(dims):
    return pl.BlockSpec(dims, lambda t: (0,) * len(dims))


def rows_of(tile, width, first=0):
    return pl.BlockSpec((tile, width), lambda t: (t + first, 0))


def columns_of(height, tile, first=0):
    return pl.BlockSpec((height, tile), lambda t: (0, t + first))


def rotated(block):
    count = lax.axis_size("chan")
    return [block] + [
        lax.ppermute(block, "chan", [(i, (i + k) % count) for i in range(count)])
        for k in range(1, count)
    ]


def gain_kernel(cot_all, gain, tails, sem):
    count, padded, pixels = cot_all.shape
    channels = padded - PAD
    copy = pltpu.make_async_copy(cot_all.at[:, channels:, :], tails, sem)
    copy.start()
    copy.wait()
    ones = jnp.ones((PAD, gain.shape[1]), BF16)
    for k in range(count):
        gain[k * channels : (k + 1) * channels, :] = dot(tails[k], ones, COLS_BY_COLS)[:channels, :]


def gain_stage(cot_all):
    count, padded, pixels = cot_all.shape
    return pl.pallas_call(
        gain_kernel,
        out_shape=shape((count * (padded - PAD), 128), F32),
        in_specs=[anywhere],
        out_specs=whole,
        scratch_shapes=[pltpu.VMEM((count, PAD, pixels), BF16), pltpu.SemaphoreType.DMA],
        compiler_params=params(60),
        cost_estimate=LIGHT,
        name="gains",
    )(cot_all)


def normalise(conv_all, gain, normed):
    count, padded, pixels = conv_all.shape
    channels = padded - PAD
    every = count * channels
    means = [jnp.sum(conv_all[k, channels:, :].astype(F32), axis=0, keepdims=True) for k in range(count)]
    mean = means[0]
    for k in range(1, count):
        mean = mean + means[k]
    mean = mean / count
    squares = jnp.zeros((8, pixels), F32)
    for k in range(count):
        moved = means[k] - mean

        def gather(index, total):
            at = pl.multiple_of(index * PAD, PAD)
            value = conv_all[k, pl.ds(at, PAD), :].astype(F32) + moved
            value = value * value
            return total + value[:8] + value[8:]

        squares = lax.fori_loop(0, channels // PAD, gather, squares, unroll=2)
    deviation = lax.rsqrt(jnp.sum(squares, axis=0, keepdims=True) / every + EPSILON)
    for k in range(count):
        moved = means[k] - mean

        def write(index, carry):
            at = pl.multiple_of(index * PAD, PAD)
            to = pl.multiple_of(k * channels + at, PAD)
            value = (conv_all[k, pl.ds(at, PAD), :].astype(F32) + moved) * deviation
            scale = gain[pl.ds(to, PAD), :]
            for p in range(pixels // 128):
                cut = slice(p * 128, (p + 1) * 128)
                normed[pl.ds(to, PAD), cut] = (value[:, cut] * scale).astype(BF16)
            return carry

        lax.fori_loop(0, channels // PAD, write, 0, unroll=2)
    return mean, deviation


def norm_kernel(conv_all, gain, normed, stats):
    mean, deviation = normalise(conv_all, gain, normed)
    row = lax.broadcasted_iota(jnp.int32, stats.shape, 0)
    stats[...] = jnp.where(row == 0, mean, jnp.where(row == 1, deviation, 0.0))


def norm_stage(conv_all, gain):
    pixels = conv_all.shape[2]
    return pl.pallas_call(
        norm_kernel,
        out_shape=(shape((gain.shape[0], pixels), BF16), shape((8, pixels), F32)),
        in_specs=[whole] * 2,
        out_specs=(whole, whole),
        compiler_params=params(32),
        cost_estimate=LIGHT,
        name="norm",
    )(conv_all, gain)


def block_kernel(steps, normed, cot_all, gain, w_expand, bias, w_reduce, hidden, grad_pre, reduced, *refs):
    blocks, (cot, reduce_sum, normed_sum) = refs[:-3], refs[-3:]
    at = pl.program_id(0)

    @pl.when(at == 0)
    def _():
        channels = cot_all.shape[1] - PAD
        for k in range(cot_all.shape[0]):
            cot[k * channels : (k + 1) * channels, :] = cot_all[k, :channels, :]
        reduce_sum[...] = jnp.zeros_like(reduce_sum)
        normed_sum[...] = jnp.zeros_like(normed_sum)

    pre = dot(w_expand[...], normed[...], ROWS_BY_COLS) + bias[...]
    back = dot(w_reduce[...], cot[...], COLS_BY_COLS)
    active, slope = gelu_parts(pre)
    active = active.astype(BF16)
    hidden[...] = active
    grad = (back * slope).astype(BF16)
    grad_pre[...] = grad
    reduce_sum[...] += dot(w_reduce[...], active, ROWS_BY_COLS)
    normed_sum[...] += dot(w_expand[...], grad, COLS_BY_COLS)

    @pl.when(at == steps - 1)
    def _():
        every, pixels = normed.shape
        reduced[...] = reduce_sum[...].astype(BF16)

        def step(index, totals):
            cut = pl.ds(pl.multiple_of(index * PAD, PAD), PAD)
            value = normed_sum[cut, :]
            first = value * jnp.concatenate([gain[cut, :]] * (pixels // gain.shape[1]), axis=1)
            cross = value * normed[cut, :].astype(F32)
            return totals[0] + first[:8] + first[8:], totals[1] + cross[:8] + cross[8:]

        totals = lax.fori_loop(0, every // PAD, step, (jnp.zeros((8, pixels), F32),) * 2, unroll=2)
        moments = stacked_rows(*[jnp.sum(total, axis=0, keepdims=True) for total in totals])
        for k, block in enumerate(blocks):
            height = block.shape[0] - PAD
            place = lax.rem(lax.axis_index("chan") + k, len(blocks)) if len(blocks) > 1 else 0
            block[:height, :] = normed_sum[pl.ds(pl.multiple_of(place * height, PAD), height), :].astype(BF16)
            block[height:, :] = moments


def block_stage(normed, cot_all, gain, w_expand, bias, w_reduce):
    count = lax.axis_size("chan")
    units, every = w_expand.shape
    pixels = normed.shape[1]
    tile = tile_of(units)
    steps = units // tile
    blocks = count if count <= 4 else 1
    return pl.pallas_call(
        functools.partial(block_kernel, steps),
        grid=(steps,),
        out_shape=(shape((units, pixels), BF16),) * 2
        + (shape((every, pixels), BF16),)
        + (shape((every // blocks + PAD, pixels), BF16),) * blocks,
        in_specs=[
            fixed(normed.shape),
            fixed(cot_all.shape),
            fixed(gain.shape),
            rows_of(tile, every),
            rows_of(tile, 1),
            columns_of(every, tile),
        ],
        out_specs=(rows_of(tile, pixels),) * 2
        + (fixed((every, pixels)),)
        + (fixed((every // blocks + PAD, pixels)),) * blocks,
        scratch_shapes=[
            pltpu.VMEM((every, pixels), BF16),
            pltpu.VMEM((every, pixels), F32),
            pltpu.VMEM((every, pixels), F32),
        ],
        compiler_params=params(60),
        cost_estimate=LIGHT,
        name="pointwise_block",
    )(normed, cot_all, gain, w_expand, bias, w_reduce)


def side_by_side(pixels):
    index = lax.axis_index("rows")
    own = pl.ds(pl.multiple_of(index * pixels, pixels), pixels)
    other = pl.ds(pl.multiple_of((1 - index) * pixels, pixels), pixels)
    return own, other


def weight_kernel(
    normed_own, normed_other, cot_own, cot_other, hidden_own, pre_own, w_expand, bias, w_reduce,
    grad_reduce, grad_expand, normed, cot, hidden, grad_pre, sems,
):
    pixels = normed_own.shape[1]
    own, other = side_by_side(pixels)

    @pl.when(pl.program_id(0) == 0)
    def _():
        copies = [
            pltpu.make_async_copy(normed_other, normed.at[:, other], sems.at[0]),
            pltpu.make_async_copy(normed_own, normed.at[:, own], sems.at[1]),
        ]
        count, padded, _ = cot_own.shape
        channels = padded - PAD
        for k in range(count):
            rows = slice(k * channels, (k + 1) * channels)
            for x, (source, cut) in enumerate(((cot_own, own), (cot_other, other))):
                copies.append(
                    pltpu.make_async_copy(source.at[k, :channels, :], cot.at[rows, cut], sems.at[2 + 2 * k + x])
                )
        for copy in copies:
            copy.start()
        for copy in copies:
            copy.wait()

    pre = dot(w_expand[...], normed[:, other], ROWS_BY_COLS) + bias[...]
    back = dot(w_reduce[...], cot[:, other], COLS_BY_COLS)
    active, slope = gelu_parts(pre)
    hidden[:, own] = hidden_own[...]
    hidden[:, other] = active.astype(BF16)
    grad_pre[:, own] = pre_own[...]
    grad_pre[:, other] = (back * slope).astype(BF16)
    grad_reduce[...] = dot(cot[...], hidden[...], ROWS_BY_ROWS).astype(BF16)
    grad_expand[...] = dot(grad_pre[...], normed[...], ROWS_BY_ROWS).astype(BF16)


def weight_gradients(part, parts, normed_own, normed_other, cot_own, cot_other, hidden, grad_pre, w_expand, bias, w_reduce):
    every, pixels = normed_own.shape
    units = w_expand.shape[0]
    tile = tile_of(units)
    steps = units // tile // parts
    first = part * steps
    return pl.pallas_call(
        weight_kernel,
        grid=(steps,),
        out_shape=(shape((every, steps * tile), BF16), shape((steps * tile, every), BF16)),
        in_specs=[anywhere] * 4
        + [
            rows_of(tile, pixels, first),
            rows_of(tile, pixels, first),
            rows_of(tile, every, first),
            rows_of(tile, 1, first),
            columns_of(every, tile, first),
        ],
        out_specs=(columns_of(every, tile), rows_of(tile, every)),
        scratch_shapes=[
            pltpu.VMEM((every, 2 * pixels), BF16),
            pltpu.VMEM((every, 2 * pixels), BF16),
            pltpu.VMEM((tile, 2 * pixels), BF16),
            pltpu.VMEM((tile, 2 * pixels), BF16),
            pltpu.SemaphoreType.DMA((2 + 2 * cot_own.shape[0],)),
        ],
        compiler_params=params(60),
        cost_estimate=LIGHT,
        name="weight_gradients",
    )(normed_own, normed_other, cot_own, cot_other, hidden, grad_pre, w_expand, bias, w_reduce)


def pair_kernel(*refs):
    mine, theirs, result = refs[0], refs[1], refs[-1]
    result[...] = (mine[...].astype(F32) + theirs[...].astype(F32)).astype(BF16)


def add_pair(part, parts, axis, mine, theirs, target):
    height, width = mine.shape
    if axis == 0:
        tile = 384 if height % 384 == 0 else tile_of(height)
        steps = height // tile
        block, dims = rows_of(tile, width), (height * parts, width)
        placed = rows_of(tile, width, part * steps)
    else:
        tile = 384 if height % 384 == 0 else tile_of(height)
        steps = height // tile
        block, dims = rows_of(tile, width), (height, width * parts)
        placed = pl.BlockSpec((tile, width), lambda t: (t, part))
    known = () if target is None else (target,)
    return pl.pallas_call(
        pair_kernel,
        grid=(steps,),
        out_shape=shape(dims, BF16),
        in_specs=[block, block] + [anywhere] * len(known),
        out_specs=placed,
        input_output_aliases={2: 0} if known else {},
        compiler_params=params(60),
        cost_estimate=LIGHT,
        name="add_pair",
    )(mine, theirs, *known)


def norm_gradient_kernel(every, centered, local, stats, gain, *refs):
    blocks, result = refs[:-1], refs[-1]
    rows, channels, width = result.shape
    mean, deviation = stats[0:1, :], stats[1:2, :]
    first = cross = 0.0
    for block in blocks:
        tail = block[channels:, :]
        first = first + unstacked(tail, 0)
        cross = cross + unstacked(tail, 1)
    first, cross = first / every, cross / every
    shift = local[0:1, :] - mean

    def step(index, carry):
        at = pl.multiple_of(index * PAD, PAD)
        cut = pl.ds(at, PAD)
        hat = (centered[cut, :] + shift) * deviation
        value = blocks[0][cut, :].astype(F32)
        for block in blocks[1:]:
            value = value + block[cut, :].astype(F32)
        value = value * gain[cut, :]
        value = ((value - first - hat * cross) * deviation).astype(BF16)
        for k in range(rows):
            result[k, cut] = value[:, k * width : (k + 1) * width]
        return carry

    lax.fori_loop(0, channels // PAD, step, 0)


def norm_gradient(every, dims, blocks, centered, local, stats, gain):
    return pl.pallas_call(
        functools.partial(norm_gradient_kernel, every),
        out_shape=shape(dims, BF16),
        in_specs=[whole] * (4 + len(blocks)),
        out_specs=whole,
        compiler_params=params(32),
        cost_estimate=LIGHT,
        name="norm_gradient",
    )(centered, local, stats, gain, *blocks)


def scattered(blocks):
    count = lax.axis_size("chan")
    if len(blocks) == 1:
        height = blocks[0].shape[0] - PAD
        total = lax.psum_scatter(blocks[0][:height], "chan", scatter_dimension=0, tiled=True)
        tail = blocks[0][height:].astype(F32)
        sums = jnp.stack([jnp.sum(tail[:3], axis=0), jnp.sum(tail[3:6], axis=0)])
        sums = lax.psum(sums, "chan")
        parts = [part for row in sums for part in pieces(row)]
        tail = jnp.zeros(tail.shape, BF16).at[:6].set(jnp.stack(parts))
        return [jnp.concatenate([total, tail])]
    return [blocks[0]] + [
        lax.ppermute(blocks[k], "chan", [(i, (i + k) % count) for i in range(count)])
        for k in range(1, count)
    ]


def after(values, *others):
    return lax.optimization_barrier((values, others))[0]


def swap(values, axis):
    return lax.ppermute(values, axis, [(0, 1), (1, 0)])


def on_device(
    image, kernel, layer_norm_weight, w_expand, bias_expand, w_reduce, layer_scale, cotangent
):
    channels, tile_rows, tile_cols = image.shape
    pixels = tile_rows * tile_cols
    every = w_reduce.shape[0]
    two_tiles = lax.axis_size("rows") == 2 and lax.axis_size("cols") == 2

    image_rows = jnp.transpose(image, (1, 0, 2))
    around = surroundings(image_rows)
    cot_rows = jnp.transpose(cotangent, (1, 0, 2))
    packed_cot = pack_cotangent(cot_rows, layer_scale[:, None], layer_norm_weight[None, :])
    cot_all = lax.all_gather(packed_cot, "chan")

    bias = bias_expand[:, None]
    packed_conv, centered, local = forward_conv(around, kernel)
    conv_all = lax.all_gather(packed_conv, "chan")
    cot_all = after(cot_all, packed_conv)
    gain = gain_stage(cot_all)
    normed, stats = norm_stage(conv_all, gain)
    ready = normed
    if two_tiles:
        cot_other = swap(cot_all, "rows")
        normed_other = swap(normed, "rows")
        ready = after(normed, cot_other)
    hidden, grad_pre, reduced, *blocks = block_stage(ready, cot_all, gain, w_expand, bias, w_reduce)
    norm_inputs = (scattered(blocks), centered, local, stats)

    if two_tiles:
        weight_inputs = (normed, normed_other, cot_all, cot_other, hidden, grad_pre, w_expand, bias, w_reduce)
        found = weight_gradients(0, 1, *weight_inputs)
        norm_inputs = after(norm_inputs, found)
    reduced = lax.psum_scatter(reduced, "chan", scatter_dimension=0, tiled=True).astype(F32)
    gradient = norm_gradient(every, image_rows.shape, *norm_inputs, layer_norm_weight[:, None])
    grad_around = surroundings(gradient)
    taps = kernel_gradient(around, gradient)
    if two_tiles:
        grad_around = after(grad_around, reduced)
    grad_rows = backward_conv(grad_around, kernel, cot_rows)
    grad_input = jnp.transpose(grad_rows, (1, 0, 2))
    if two_tiles:
        taps = after(taps, grad_rows)
        taps = taps + swap(taps, "cols")
        taps = taps + swap(taps, "rows")
        theirs = [swap(after(mine, gradient), "cols") for mine in found]
        grad_reduce, grad_expand = [add_pair(0, 1, 0, *pair, None) for pair in zip(found, theirs)]
    else:
        taps = lax.psum(taps, ("rows", "cols"))
        cot = cot_all[:, :channels, :].reshape(every, pixels)
        grad_reduce = dot(cot, hidden, ROWS_BY_ROWS).astype(BF16)
        grad_expand = dot(grad_pre, normed, ROWS_BY_ROWS).astype(BF16)
        grad_reduce, grad_expand = lax.psum((grad_reduce, grad_expand), ("rows", "cols"))
    taps = taps[:, : KS * KS]

    output = (
        image.reshape(channels, pixels).astype(F32) + layer_scale[:, None] * reduced
    ).astype(BF16).reshape(image.shape)
    return output, grad_input, grad_expand, grad_reduce, taps


def solution(mesh):
    placed = (
        P("chan", ("groups", "rows"), "cols"),
        P("chan", None),
        P("chan"),
        P("chan", None),
        P("chan"),
        P(None, "chan"),
        P("chan"),
        P("chan", ("groups", "rows"), "cols"),
    )
    return jax.shard_map(
        on_device,
        mesh=mesh,
        in_specs=placed,
        out_specs=(
            P("chan", ("groups", "rows"), "cols"),
            P("chan", ("groups", "rows"), "cols"),
            P(("groups", "chan"), None),
            P("groups", "chan"),
            P(("groups", "chan"), None),
        ),
        check_vma=False,
    )
```

```python
import functools

import jax
import jax.numpy as jnp
from jax import lax
from jax.experimental import pallas as pl
from jax.experimental.pallas import tpu as pltpu
from jax.sharding import PartitionSpec as P

KS = 7
HALF = KS // 2
PAD = 16
EPSILON = 1e-06
MIB = 1024 * 1024
F32 = jnp.float32
BF16 = jnp.bfloat16

whole = pl.BlockSpec(memory_space=pltpu.VMEM)
anywhere = pl.BlockSpec(memory_space=pl.ANY)
LIGHT = pl.CostEstimate(flops=1000, bytes_accessed=1000, transcendentals=0)


def params(mib):
    return pltpu.CompilerParams(vmem_limit_bytes=mib * MIB)


def shape(dims, dtype):
    return jax.ShapeDtypeStruct(dims, dtype)


def pieces(values):
    high = values.astype(BF16)
    rest = values - high.astype(F32)
    middle = rest.astype(BF16)
    low = (rest - middle.astype(F32)).astype(BF16)
    return high, middle, low


def stacked_rows(*rows):
    width = rows[0].shape[1]
    row = lax.broadcasted_iota(jnp.int32, (PAD, width), 0)
    block = jnp.zeros((PAD, width), F32)
    for first, values in enumerate(rows):
        for index, part in enumerate(pieces(values)):
            block = jnp.where(row == 3 * first + index, part.astype(F32), block)
    return block.astype(BF16)


def unstacked(block, first):
    return jnp.sum(block[3 * first : 3 * first + 3, :].astype(F32), axis=0, keepdims=True)


def from_sides(low_source, high_source, axis):
    count = lax.axis_size(axis)
    if count == 2:
        index = lax.axis_index(axis)
        sent = jnp.where(index == 0, low_source, high_source)
        got = lax.ppermute(sent, axis, [(0, 1), (1, 0)])
        return got, got
    forward = [(i, i + 1) for i in range(count - 1)]
    backward = [(i + 1, i) for i in range(count - 1)]
    return lax.ppermute(low_source, axis, forward), lax.ppermute(high_source, axis, backward)


def edges(block, axis):
    count = lax.axis_size(axis)
    if count == 2:
        return lax.ppermute(block, axis, [(0, 1), (1, 0)])
    low, high = from_sides(block, block, axis)
    width = block.shape[-1]
    lane = lax.broadcasted_iota(jnp.int32, block.shape, block.ndim - 1)
    return jnp.where(lane < width // 2, high, low)


def surroundings(block, before_corner=None):
    rows = block.shape[0]
    above, below = from_sides(block[rows - HALF :], block[:HALF], "rows")
    side = edges(block, "cols")
    if before_corner is not None:
        above, below = after((above, below), before_corner)
    if lax.axis_size("rows") == 2:
        corner = edges(above, "cols")
        return block, above, below, side, corner, corner
    return block, above, below, side, edges(above, "cols"), edges(below, "cols")


def flag(test):
    return jnp.where(test, 1.0, 0.0).astype(F32)


def fill_shifts(shifts):
    width = shifts.shape[0] // 2
    col = lax.axis_index("cols")
    has_right, has_left = flag(col < lax.axis_size("cols") - 1), flag(col > 0)
    source = lax.broadcasted_iota(jnp.int32, (width, width), 0)
    target = lax.broadcasted_iota(jnp.int32, (width, width), 1)
    for tap in range(KS):
        cut = slice(tap * width, (tap + 1) * width)
        wanted = target + (tap - HALF)
        shifts[:width, cut] = jnp.where(source == wanted, 1.0, 0.0).astype(BF16)
        right = jnp.where(source + width == wanted, has_right, 0.0)
        left = jnp.where(source - width == wanted, has_left, 0.0)
        shifts[width:, cut] = (right + left).astype(BF16)


def shifted_rows(refs, shifts, at, count):
    block, above, below, side, above_side, below_side = refs
    row = lax.axis_index("rows")
    has_above = flag(row > 0).astype(BF16)
    has_below = flag(row < lax.axis_size("rows") - 1).astype(BF16)
    rows = block.shape[0]
    cut = pl.ds(at, count)
    found = [jnp.concatenate([above[k, cut], above_side[k, cut]], axis=1) * has_above for k in range(HALF)]
    found += [jnp.concatenate([block[k, cut], side[k, cut]], axis=1) for k in range(rows)]
    found += [jnp.concatenate([below[k, cut], below_side[k, cut]], axis=1) * has_below for k in range(HALF)]
    return dot(jnp.concatenate(found, axis=0), shifts[...], ROWS_BY_COLS)


def convolve(refs, shifts, taps, at, count, flipped):
    rows, _, width = refs[0].shape
    moved = shifted_rows(refs, shifts, at, count)
    sums = [None] * rows
    for tap_col in range(KS):
        near = [
            moved[k * count : (k + 1) * count, tap_col * width : (tap_col + 1) * width]
            for k in range(rows + KS - 1)
        ]
        for tap_row in range(KS):
            tap = tap_row * KS + tap_col
            tap = KS * KS - 1 - tap if flipped else tap
            weight = jnp.broadcast_to(taps[:, tap : tap + 1], (count, width))
            for k in range(rows):
                term = weight * near[k + tap_row]
                sums[k] = term if sums[k] is None else sums[k] + term
    return sums


def forward_conv_kernel(block, above, below, side, above_side, below_side, kernel, packed, centered, local, shifts):
    refs = (block, above, below, side, above_side, below_side)
    rows, channels, width = block.shape
    fill_shifts(shifts)

    def step(index, totals):
        at = pl.multiple_of(index * PAD, PAD)
        sums = convolve(refs, shifts, kernel[pl.ds(at, PAD), :], at, PAD, False)
        for k in range(rows):
            centered[pl.ds(at, PAD), k * width : (k + 1) * width] = sums[k]
        return tuple(total + value[:8] + value[8:] for total, value in zip(totals, sums))

    totals = lax.fori_loop(
        0, channels // PAD, step, tuple(jnp.zeros((8, width), F32) for _ in range(rows)), unroll=2
    )
    mean = jnp.concatenate([jnp.sum(total, axis=0, keepdims=True) for total in totals], axis=1) / channels
    local[...] = jnp.broadcast_to(mean, local.shape)

    def finish(index, carry):
        at = pl.multiple_of(index * PAD, PAD)
        value = centered[pl.ds(at, PAD), :] - mean
        centered[pl.ds(at, PAD), :] = value
        packed[pl.ds(at, PAD), :] = value.astype(BF16)
        return carry

    lax.fori_loop(0, channels // PAD, finish, 0, unroll=2)
    packed[channels:, :] = stacked_rows(mean)


def shift_scratch(width):
    return [pltpu.VMEM((2 * width, KS * width), BF16)]


def forward_conv(around, kernel):
    rows, channels, width = around[0].shape
    pixels = rows * width
    return pl.pallas_call(
        forward_conv_kernel,
        out_shape=(
            shape((channels + PAD, pixels), BF16),
            shape((channels, pixels), F32),
            shape((8, pixels), F32),
        ),
        in_specs=[whole] * 7,
        out_specs=(whole,) * 3,
        scratch_shapes=shift_scratch(width),
        compiler_params=params(32),
        cost_estimate=LIGHT,
        name="conv_forward",
    )(*around, kernel)


def backward_conv_kernel(block, above, below, side, above_side, below_side, kernel, cotangent, result, shifts):
    refs = (block, above, below, side, above_side, below_side)
    rows, channels, width = block.shape
    fill_shifts(shifts)

    def step(index, carry):
        at = pl.multiple_of(index * PAD, PAD)
        sums = convolve(refs, shifts, kernel[pl.ds(at, PAD), :], at, PAD, True)
        for k in range(rows):
            result[k, pl.ds(at, PAD)] = (sums[k] + cotangent[k, pl.ds(at, PAD)].astype(F32)).astype(BF16)
        return carry

    lax.fori_loop(0, channels // PAD, step, 0, unroll=2)


def backward_conv(around, kernel, cotangent):
    return pl.pallas_call(
        backward_conv_kernel,
        out_shape=shape(cotangent.shape, BF16),
        in_specs=[whole] * 8,
        out_specs=whole,
        scratch_shapes=shift_scratch(cotangent.shape[2]),
        compiler_params=params(32),
        cost_estimate=LIGHT,
        name="conv_backward",
    )(*around, kernel, cotangent)


def kernel_gradient_kernel(block, above, below, side, above_side, below_side, gradient, result, shifts):
    refs = (block, above, below, side, above_side, below_side)
    rows, channels, width = block.shape
    fill_shifts(shifts)

    def step(index, carry):
        at = pl.multiple_of(index * PAD, PAD)
        moved = shifted_rows(refs, shifts, at, PAD)
        lane = lax.broadcasted_iota(jnp.int32, (PAD, width), 1)
        grads = [gradient[k, pl.ds(at, PAD)].astype(F32) for k in range(rows)]
        sums = jnp.zeros((PAD, width), F32)
        for tap_col in range(KS):
            near = [
                moved[k * PAD : (k + 1) * PAD, tap_col * width : (tap_col + 1) * width]
                for k in range(rows + KS - 1)
            ]
            for tap_row in range(KS):
                total = grads[0] * near[tap_row]
                for k in range(1, rows):
                    total = total + grads[k] * near[k + tap_row]
                tap = tap_row * KS + tap_col
                sums = jnp.where(lane == tap, jnp.sum(total, axis=1, keepdims=True), sums)
        result[pl.ds(at, PAD), :] = sums
        return carry

    lax.fori_loop(0, channels // PAD, step, 0, unroll=2)


def kernel_gradient(around, gradient):
    rows, channels, width = gradient.shape
    return pl.pallas_call(
        kernel_gradient_kernel,
        out_shape=shape((channels, width), F32),
        in_specs=[whole] * 7,
        out_specs=whole,
        scratch_shapes=shift_scratch(width),
        compiler_params=params(32),
        cost_estimate=LIGHT,
        name="kernel_gradient",
    )(*around, gradient)


def pack_kernel(cotangent, scale, gain, packed):
    rows, channels, width = cotangent.shape
    for k in range(rows):
        packed[:channels, k * width : (k + 1) * width] = (
            cotangent[k].astype(F32) * scale[...]
        ).astype(BF16)
    packed[channels:, :] = jnp.zeros((PAD, rows * width), BF16)
    packed[channels:, :channels] = stacked_rows(gain[...])


def pack_cotangent(cotangent, scale, gain):
    rows, channels, width = cotangent.shape
    return pl.pallas_call(
        pack_kernel,
        out_shape=shape((channels + PAD, rows * width), BF16),
        in_specs=[whole] * 3,
        out_specs=whole,
        compiler_params=params(32),
        name="pack_cotangent",
    )(cotangent, scale, gain)


def gelu_parts(values):
    cdf = 0.5 * (1.0 + lax.erf(values * 0.7071067811865476))
    slope = cdf + values * jnp.exp(-0.5 * values * values) * 0.3989422804014327
    return values * cdf, slope


ROWS_BY_COLS = (((1,), (0,)), ((), ()))
COLS_BY_COLS = (((0,), (0,)), ((), ()))
ROWS_BY_ROWS = (((1,), (1,)), ((), ()))


def dot(left, right, dims):
    return lax.dot_general(left, right, dims, preferred_element_type=F32)


def tile_of(hidden_units):
    for size in (256, 128):
        if hidden_units % size == 0:
            return size
    return hidden_units


def fixed(dims):
    return pl.BlockSpec(dims, lambda t: (0,) * len(dims))


def rows_of(tile, width, first=0):
    return pl.BlockSpec((tile, width), lambda t: (t + first, 0))


def columns_of(height, tile, first=0):
    return pl.BlockSpec((height, tile), lambda t: (0, t + first))


def rotated(block):
    count = lax.axis_size("chan")
    return [block] + [
        lax.ppermute(block, "chan", [(i, (i + k) % count) for i in range(count)])
        for k in range(1, count)
    ]


def cot_kernel(cot_all, w_reduce, bias, gain, wide_bias, back, matrix):
    count, padded, pixels = cot_all.shape
    channels = padded - PAD

    @pl.when(pl.program_id(0) == 0)
    def _():
        ones = jnp.ones((PAD, gain.shape[1]), BF16)
        wide_bias[...] = dot(stacked_rows(bias[...]), ones, COLS_BY_COLS)
        for k in range(count):
            cut = slice(k * channels, (k + 1) * channels)
            matrix[cut, :] = cot_all[k, :channels, :]
            gain[cut, :] = dot(cot_all[k, channels:, :], ones, COLS_BY_COLS)[:channels, :]

    back[...] = dot(w_reduce[...], matrix[...], COLS_BY_COLS)


def cot_stage(cot_all, w_reduce, bias):
    pixels = cot_all.shape[2]
    every, units = w_reduce.shape
    tile = tile_of(units)
    return pl.pallas_call(
        cot_kernel,
        grid=(units // tile,),
        out_shape=(shape((every, 128), F32), shape((units, 128), F32), shape((units, pixels), F32)),
        in_specs=[fixed(cot_all.shape), columns_of(every, tile), fixed((1, units))],
        out_specs=(fixed((every, 128)), fixed((units, 128)), rows_of(tile, pixels)),
        scratch_shapes=[pltpu.VMEM((every, pixels), BF16)],
        compiler_params=params(60),
        cost_estimate=LIGHT,
        name="cotangent_stage",
    )(cot_all, w_reduce, bias[None, :])


def widened(values, pixels):
    return jnp.concatenate([values] * (pixels // values.shape[1]), axis=1)


def normalise(conv_all, gain, normed):
    count, padded, pixels = conv_all.shape
    channels = padded - PAD
    every = count * channels
    means = [jnp.sum(conv_all[k, channels:, :].astype(F32), axis=0, keepdims=True) for k in range(count)]
    mean = means[0]
    for k in range(1, count):
        mean = mean + means[k]
    mean = mean / count
    squares = jnp.zeros((8, pixels), F32)
    for k in range(count):
        moved = means[k] - mean

        def gather(index, total):
            at = pl.multiple_of(index * PAD, PAD)
            value = conv_all[k, pl.ds(at, PAD), :].astype(F32) + moved
            value = value * value
            return total + value[:8] + value[8:]

        squares = lax.fori_loop(0, channels // PAD, gather, squares, unroll=2)
    deviation = lax.rsqrt(jnp.sum(squares, axis=0, keepdims=True) / every + EPSILON)
    for k in range(count):
        moved = means[k] - mean

        def write(index, carry):
            at = pl.multiple_of(index * PAD, PAD)
            to = pl.multiple_of(k * channels + at, PAD)
            value = (conv_all[k, pl.ds(at, PAD), :].astype(F32) + moved) * deviation
            scale = gain[pl.ds(to, PAD), :]
            for p in range(pixels // 128):
                cut = slice(p * 128, (p + 1) * 128)
                normed[pl.ds(to, PAD), cut] = (value[:, cut] * scale).astype(BF16)
            return carry

        lax.fori_loop(0, channels // PAD, write, 0, unroll=2)
    return mean, deviation


def norm_kernel(conv_all, gain, normed, stats):
    mean, deviation = normalise(conv_all, gain, normed)
    row = lax.broadcasted_iota(jnp.int32, stats.shape, 0)
    stats[...] = jnp.where(row == 0, mean, jnp.where(row == 1, deviation, 0.0))


def norm_stage(conv_all, gain):
    pixels = conv_all.shape[2]
    return pl.pallas_call(
        norm_kernel,
        out_shape=(shape((gain.shape[0], pixels), BF16), shape((8, pixels), F32)),
        in_specs=[whole] * 2,
        out_specs=(whole, whole),
        compiler_params=params(32),
        cost_estimate=LIGHT,
        name="norm",
    )(conv_all, gain)


def block_kernel(steps, normed, gain, w_expand, bias, back, hidden, grad_pre, *refs):
    blocks, normed_sum = refs[:-1], refs[-1]
    at = pl.program_id(0)

    @pl.when(at == 0)
    def _():
        normed_sum[...] = jnp.zeros_like(normed_sum)

    pre = dot(w_expand[...], normed[...], ROWS_BY_COLS) + widened(bias[...], normed.shape[1])
    active, slope = gelu_parts(pre)
    hidden[...] = active.astype(BF16)
    grad = (back[...] * slope).astype(BF16)
    grad_pre[...] = grad
    normed_sum[...] += dot(w_expand[...], grad, COLS_BY_COLS)

    @pl.when(at == steps - 1)
    def _():
        every, pixels = normed.shape
        def step(index, totals):
            cut = pl.ds(pl.multiple_of(index * PAD, PAD), PAD)
            value = normed_sum[cut, :]
            first = value * widened(gain[cut, :], pixels)
            cross = value * normed[cut, :].astype(F32)
            return totals[0] + first[:8] + first[8:], totals[1] + cross[:8] + cross[8:]

        totals = lax.fori_loop(0, every // PAD, step, (jnp.zeros((8, pixels), F32),) * 2, unroll=2)
        moments = stacked_rows(*[jnp.sum(total, axis=0, keepdims=True) for total in totals])
        for k, block in enumerate(blocks):
            height = block.shape[0] - PAD
            place = lax.rem(lax.axis_index("chan") + k, len(blocks)) if len(blocks) > 1 else 0
            block[:height, :] = normed_sum[pl.ds(pl.multiple_of(place * height, PAD), height), :].astype(BF16)
            block[height:, :] = moments


def block_stage(normed, gain, w_expand, bias, back):
    count = lax.axis_size("chan")
    units, every = w_expand.shape
    pixels = normed.shape[1]
    tile = tile_of(units)
    steps = units // tile
    blocks = count if count <= 4 else 1
    return pl.pallas_call(
        functools.partial(block_kernel, steps),
        grid=(steps,),
        out_shape=(shape((units, pixels), BF16),) * 2
        + (shape((every // blocks + PAD, pixels), BF16),) * blocks,
        in_specs=[
            fixed(normed.shape),
            fixed(gain.shape),
            rows_of(tile, every),
            rows_of(tile, 128),
            rows_of(tile, pixels),
        ],
        out_specs=(rows_of(tile, pixels),) * 2 + (fixed((every // blocks + PAD, pixels)),) * blocks,
        scratch_shapes=[pltpu.VMEM((every, pixels), F32)],
        compiler_params=params(60),
        cost_estimate=LIGHT,
        name="pointwise_block",
    )(normed, gain, w_expand, bias, back)


def reduced_kernel(weight, hidden, result):
    result[...] = dot(weight[...], hidden[...], ROWS_BY_COLS).astype(BF16)


def reduce_product(w_reduce, hidden):
    every, units = w_reduce.shape
    pixels = hidden.shape[1]
    tile = 512 if every % 512 == 0 else tile_of(every)
    return pl.pallas_call(
        reduced_kernel,
        grid=(every // tile,),
        out_shape=shape((every, pixels), BF16),
        in_specs=[rows_of(tile, units), fixed(hidden.shape)],
        out_specs=rows_of(tile, pixels),
        compiler_params=params(60),
        cost_estimate=LIGHT,
        name="reduced_product",
    )(w_reduce, hidden)


def unpack(cot_all, target):
    channels = cot_all.shape[1] - PAD
    for k in range(cot_all.shape[0]):
        target[k * channels : (k + 1) * channels, :] = cot_all[k, :channels, :]


def own_tile_kernel(normed, cot_all, hidden, grad_pre, grad_reduce, grad_expand, cot):
    @pl.when(pl.program_id(0) == 0)
    def _():
        unpack(cot_all, cot)

    grad_reduce[...] = dot(cot[...], hidden[...], ROWS_BY_ROWS).astype(BF16)
    grad_expand[...] = dot(grad_pre[...], normed[...], ROWS_BY_ROWS).astype(BF16)


def own_tile_gradients(normed, cot_all, hidden, grad_pre):
    every, pixels = normed.shape
    units = hidden.shape[0]
    tile = tile_of(units)
    return pl.pallas_call(
        own_tile_kernel,
        grid=(units // tile,),
        out_shape=(shape((every, units), BF16), shape((units, every), BF16)),
        in_specs=[fixed(normed.shape), fixed(cot_all.shape), rows_of(tile, pixels), rows_of(tile, pixels)],
        out_specs=(columns_of(every, tile), rows_of(tile, every)),
        scratch_shapes=[pltpu.VMEM((every, pixels), BF16)],
        compiler_params=params(60),
        cost_estimate=LIGHT,
        name="own_tile_gradients",
    )(normed, cot_all, hidden, grad_pre)


def plus(first, product):
    return (first.astype(F32) + product.astype(BF16).astype(F32)).astype(BF16)


def other_tile_kernel(
    normed, cot_all, reduce_own, expand_own, w_expand, bias, w_reduce, grad_reduce, grad_expand, cot
):
    @pl.when(pl.program_id(0) == 0)
    def _():
        unpack(cot_all, cot)

    pre = dot(w_expand[...], normed[...], ROWS_BY_COLS) + widened(bias[...], normed.shape[1])
    back = dot(w_reduce[...], cot[...], COLS_BY_COLS)
    active, slope = gelu_parts(pre)
    grad_pre = (back * slope).astype(BF16)
    grad_reduce[...] = plus(reduce_own[...], dot(cot[...], active.astype(BF16), ROWS_BY_ROWS))
    grad_expand[...] = plus(expand_own[...], dot(grad_pre, normed[...], ROWS_BY_ROWS))


def two_tile_gradients(normed, cot_all, reduce_own, expand_own, w_expand, bias, w_reduce):
    every, pixels = normed.shape
    units = w_expand.shape[0]
    tile = tile_of(units)
    return pl.pallas_call(
        other_tile_kernel,
        grid=(units // tile,),
        out_shape=(shape((every, units), BF16), shape((units, every), BF16)),
        in_specs=[
            fixed(normed.shape),
            fixed(cot_all.shape),
            columns_of(every, tile),
            rows_of(tile, every),
            rows_of(tile, every),
            rows_of(tile, 128),
            columns_of(every, tile),
        ],
        out_specs=(columns_of(every, tile), rows_of(tile, every)),
        scratch_shapes=[pltpu.VMEM((every, pixels), BF16)],
        compiler_params=params(60),
        cost_estimate=LIGHT,
        name="two_tile_gradients",
    )(normed, cot_all, reduce_own, expand_own, w_expand, bias, w_reduce)


def pair_kernel(*refs):
    mine, theirs, result = refs[0], refs[1], refs[-1]
    result[...] = (mine[...].astype(F32) + theirs[...].astype(F32)).astype(BF16)


def add_pair(part, parts, axis, mine, theirs, target):
    height, width = mine.shape
    if axis == 0:
        tile = 384 if height % 384 == 0 else tile_of(height)
        steps = height // tile
        block, dims = rows_of(tile, width), (height * parts, width)
        placed = rows_of(tile, width, part * steps)
    else:
        tile = 384 if height % 384 == 0 else tile_of(height)
        steps = height // tile
        block, dims = rows_of(tile, width), (height, width * parts)
        placed = pl.BlockSpec((tile, width), lambda t: (t, part))
    known = () if target is None else (target,)
    return pl.pallas_call(
        pair_kernel,
        grid=(steps,),
        out_shape=shape(dims, BF16),
        in_specs=[block, block] + [anywhere] * len(known),
        out_specs=placed,
        input_output_aliases={2: 0} if known else {},
        compiler_params=params(60),
        cost_estimate=LIGHT,
        name="add_pair",
    )(mine, theirs, *known)


def norm_gradient_kernel(every, centered, local, stats, gain, *refs):
    blocks, result = refs[:-1], refs[-1]
    rows, channels, width = result.shape
    mean, deviation = stats[0:1, :], stats[1:2, :]
    first = cross = 0.0
    for block in blocks:
        tail = block[channels:, :]
        first = first + unstacked(tail, 0)
        cross = cross + unstacked(tail, 1)
    first, cross = first / every, cross / every
    shift = local[0:1, :] - mean
    own = lax.axis_index("chan") * channels

    def step(index, carry):
        at = pl.multiple_of(index * PAD, PAD)
        cut = pl.ds(at, PAD)
        hat = (centered[cut, :] + shift) * deviation
        value = blocks[0][cut, :].astype(F32)
        for block in blocks[1:]:
            value = value + block[cut, :].astype(F32)
        value = value * widened(gain[pl.ds(pl.multiple_of(own + at, PAD), PAD), :], value.shape[1])
        value = ((value - first - hat * cross) * deviation).astype(BF16)
        for k in range(rows):
            result[k, cut] = value[:, k * width : (k + 1) * width]
        return carry

    lax.fori_loop(0, channels // PAD, step, 0)


def norm_gradient(every, dims, blocks, centered, local, stats, gain):
    return pl.pallas_call(
        functools.partial(norm_gradient_kernel, every),
        out_shape=shape(dims, BF16),
        in_specs=[whole] * (4 + len(blocks)),
        out_specs=whole,
        compiler_params=params(32),
        cost_estimate=LIGHT,
        name="norm_gradient",
    )(centered, local, stats, gain, *blocks)


def scattered(blocks):
    count = lax.axis_size("chan")
    if len(blocks) == 1:
        height = blocks[0].shape[0] - PAD
        total = lax.psum_scatter(blocks[0][:height], "chan", scatter_dimension=0, tiled=True)
        tail = blocks[0][height:].astype(F32)
        sums = jnp.stack([jnp.sum(tail[:3], axis=0), jnp.sum(tail[3:6], axis=0)])
        sums = lax.psum(sums, "chan")
        parts = [part for row in sums for part in pieces(row)]
        tail = jnp.zeros(tail.shape, BF16).at[:6].set(jnp.stack(parts))
        return [jnp.concatenate([total, tail])]
    return [blocks[0]] + [
        lax.ppermute(blocks[k], "chan", [(i, (i + k) % count) for i in range(count)])
        for k in range(1, count)
    ]


def after(values, *others):
    return lax.optimization_barrier((values, others))[0]


def swap(values, axis):
    return lax.ppermute(values, axis, [(0, 1), (1, 0)])


def on_device(
    image, kernel, layer_norm_weight, w_expand, bias_expand, w_reduce, layer_scale, cotangent
):
    channels, tile_rows, tile_cols = image.shape
    pixels = tile_rows * tile_cols
    every = w_reduce.shape[0]
    two_tiles = lax.axis_size("rows") == 2 and lax.axis_size("cols") == 2

    image_rows = jnp.transpose(image, (1, 0, 2))
    around = surroundings(image_rows)
    cot_rows = jnp.transpose(cotangent, (1, 0, 2))
    packed_cot = pack_cotangent(cot_rows, layer_scale[:, None], layer_norm_weight[None, :])
    cot_all = lax.all_gather(packed_cot, "chan")

    packed_conv, centered, local = forward_conv(around, kernel)
    conv_all = lax.all_gather(packed_conv, "chan")
    cot_all, bias = after((cot_all, bias_expand), packed_conv)
    gain, bias, back = cot_stage(cot_all, w_reduce, bias)
    normed, stats = norm_stage(conv_all, gain)
    ready = normed
    if two_tiles:
        cot_other = swap(cot_all, "rows")
        normed_other = swap(normed, "rows")
        ready = after(normed, cot_other)
    hidden, grad_pre, *blocks = block_stage(ready, gain, w_expand, bias, back)
    norm_inputs = (scattered(blocks), centered, local, stats)
    product = reduce_product(w_reduce, hidden)
    reduced = lax.psum_scatter(product, "chan", scatter_dimension=0, tiled=True)

    if two_tiles:
        own = own_tile_gradients(normed, cot_all, after(hidden, product), grad_pre)
        found = two_tile_gradients(normed_other, cot_other, *own, w_expand, bias, w_reduce)
        norm_inputs = after(norm_inputs, found)
    gradient = norm_gradient(every, image_rows.shape, *norm_inputs, gain)
    taps = kernel_gradient(around, gradient)
    grad_around = surroundings(gradient, taps if two_tiles else None)
    if two_tiles:
        theirs = [swap(after(mine, gradient), "cols") for mine in found]
        grad_reduce = add_pair(0, 1, 0, found[0], theirs[0], None)
        grad_around = after(grad_around, grad_reduce)
    grad_rows = backward_conv(grad_around, kernel, cot_rows)
    grad_input = jnp.transpose(grad_rows, (1, 0, 2))
    if two_tiles:
        taps = after(taps, grad_rows)
        taps = taps + swap(taps, "cols")
        taps = taps + swap(taps, "rows")
        grad_expand = add_pair(0, 1, 0, found[1], theirs[1], None)
        reduced = after(reduced, grad_expand, taps)
    else:
        taps = lax.psum(taps, ("rows", "cols"))
        cot = cot_all[:, :channels, :].reshape(every, pixels)
        grad_reduce = dot(cot, hidden, ROWS_BY_ROWS).astype(BF16)
        grad_expand = dot(grad_pre, normed, ROWS_BY_ROWS).astype(BF16)
        grad_reduce, grad_expand = lax.psum((grad_reduce, grad_expand), ("rows", "cols"))
    taps = taps[:, : KS * KS]

    output = (
        image.reshape(channels, pixels).astype(F32) + layer_scale[:, None] * reduced.astype(F32)
    ).astype(BF16).reshape(image.shape)
    return output, grad_input, grad_expand, grad_reduce, taps


def solution(mesh):
    placed = (
        P("chan", ("groups", "rows"), "cols"),
        P("chan", None),
        P("chan"),
        P("chan", None),
        P("chan"),
        P(None, "chan"),
        P("chan"),
        P("chan", ("groups", "rows"), "cols"),
    )
    return jax.shard_map(
        on_device,
        mesh=mesh,
        in_specs=placed,
        out_specs=(
            P("chan", ("groups", "rows"), "cols"),
            P("chan", ("groups", "rows"), "cols"),
            P(("groups", "chan"), None),
            P("groups", "chan"),
            P(("groups", "chan"), None),
        ),
        check_vma=False,
    )
```

```python
import functools

import jax
import jax.numpy as jnp
from jax import lax
from jax.experimental import pallas as pl
from jax.experimental.pallas import tpu as pltpu
from jax.sharding import PartitionSpec as P

KS = 7
HALF = KS // 2
PAD = 16
EPSILON = 1e-06
MIB = 1024 * 1024
F32 = jnp.float32
BF16 = jnp.bfloat16

whole = pl.BlockSpec(memory_space=pltpu.VMEM)
anywhere = pl.BlockSpec(memory_space=pl.ANY)
LIGHT = pl.CostEstimate(flops=1000, bytes_accessed=1000, transcendentals=0)


def params(mib):
    return pltpu.CompilerParams(vmem_limit_bytes=mib * MIB)


def shape(dims, dtype):
    return jax.ShapeDtypeStruct(dims, dtype)


def pieces(values):
    high = values.astype(BF16)
    rest = values - high.astype(F32)
    middle = rest.astype(BF16)
    low = (rest - middle.astype(F32)).astype(BF16)
    return high, middle, low


def stacked_rows(*rows):
    width = rows[0].shape[1]
    row = lax.broadcasted_iota(jnp.int32, (PAD, width), 0)
    block = jnp.zeros((PAD, width), F32)
    for first, values in enumerate(rows):
        for index, part in enumerate(pieces(values)):
            block = jnp.where(row == 3 * first + index, part.astype(F32), block)
    return block.astype(BF16)


def unstacked(block, first):
    return jnp.sum(block[3 * first : 3 * first + 3, :].astype(F32), axis=0, keepdims=True)


def from_sides(low_source, high_source, axis):
    count = lax.axis_size(axis)
    if count == 2:
        index = lax.axis_index(axis)
        sent = jnp.where(index == 0, low_source, high_source)
        got = lax.ppermute(sent, axis, [(0, 1), (1, 0)])
        return got, got
    forward = [(i, i + 1) for i in range(count - 1)]
    backward = [(i + 1, i) for i in range(count - 1)]
    return lax.ppermute(low_source, axis, forward), lax.ppermute(high_source, axis, backward)


def edges(block, axis):
    count = lax.axis_size(axis)
    if count == 2:
        return lax.ppermute(block, axis, [(0, 1), (1, 0)])
    low, high = from_sides(block, block, axis)
    width = block.shape[-1]
    lane = lax.broadcasted_iota(jnp.int32, block.shape, block.ndim - 1)
    return jnp.where(lane < width // 2, high, low)


def surroundings(block, before_corner=None):
    rows = block.shape[0]
    above, below = from_sides(block[rows - HALF :], block[:HALF], "rows")
    side = edges(block, "cols")
    if before_corner is not None:
        above, below = after((above, below), before_corner)
    if lax.axis_size("rows") == 2:
        corner = edges(above, "cols")
        return block, above, below, side, corner, corner
    return block, above, below, side, edges(above, "cols"), edges(below, "cols")


def flag(test):
    return jnp.where(test, 1.0, 0.0).astype(F32)


def fill_shifts(shifts):
    width = shifts.shape[0] // 2
    col = lax.axis_index("cols")
    has_right, has_left = flag(col < lax.axis_size("cols") - 1), flag(col > 0)
    source = lax.broadcasted_iota(jnp.int32, (width, width), 0)
    target = lax.broadcasted_iota(jnp.int32, (width, width), 1)
    for tap in range(KS):
        cut = slice(tap * width, (tap + 1) * width)
        wanted = target + (tap - HALF)
        shifts[:width, cut] = jnp.where(source == wanted, 1.0, 0.0).astype(BF16)
        right = jnp.where(source + width == wanted, has_right, 0.0)
        left = jnp.where(source - width == wanted, has_left, 0.0)
        shifts[width:, cut] = (right + left).astype(BF16)


def shifted_rows(refs, shifts, at, count):
    block, above, below, side, above_side, below_side = refs
    row = lax.axis_index("rows")
    has_above = flag(row > 0).astype(BF16)
    has_below = flag(row < lax.axis_size("rows") - 1).astype(BF16)
    rows = block.shape[0]
    cut = pl.ds(at, count)
    found = [jnp.concatenate([above[k, cut], above_side[k, cut]], axis=1) * has_above for k in range(HALF)]
    found += [jnp.concatenate([block[k, cut], side[k, cut]], axis=1) for k in range(rows)]
    found += [jnp.concatenate([below[k, cut], below_side[k, cut]], axis=1) * has_below for k in range(HALF)]
    return dot(jnp.concatenate(found, axis=0), shifts[...], ROWS_BY_COLS)


def convolve(refs, shifts, taps, at, count, flipped):
    rows, _, width = refs[0].shape
    moved = shifted_rows(refs, shifts, at, count)
    sums = [None] * rows
    for tap_col in range(KS):
        near = [
            moved[k * count : (k + 1) * count, tap_col * width : (tap_col + 1) * width]
            for k in range(rows + KS - 1)
        ]
        for tap_row in range(KS):
            tap = tap_row * KS + tap_col
            tap = KS * KS - 1 - tap if flipped else tap
            weight = jnp.broadcast_to(taps[:, tap : tap + 1], (count, width))
            for k in range(rows):
                term = weight * near[k + tap_row]
                sums[k] = term if sums[k] is None else sums[k] + term
    return sums


def forward_conv_kernel(block, above, below, side, above_side, below_side, kernel, packed, centered, local, shifts):
    refs = (block, above, below, side, above_side, below_side)
    rows, channels, width = block.shape
    fill_shifts(shifts)

    def step(index, totals):
        at = pl.multiple_of(index * PAD, PAD)
        sums = convolve(refs, shifts, kernel[pl.ds(at, PAD), :], at, PAD, False)
        for k in range(rows):
            centered[pl.ds(at, PAD), k * width : (k + 1) * width] = sums[k]
        return tuple(total + value[:8] + value[8:] for total, value in zip(totals, sums))

    totals = lax.fori_loop(
        0, channels // PAD, step, tuple(jnp.zeros((8, width), F32) for _ in range(rows)), unroll=2
    )
    mean = jnp.concatenate([jnp.sum(total, axis=0, keepdims=True) for total in totals], axis=1) / channels
    local[...] = jnp.broadcast_to(mean, local.shape)

    def finish(index, carry):
        at = pl.multiple_of(index * PAD, PAD)
        value = centered[pl.ds(at, PAD), :] - mean
        centered[pl.ds(at, PAD), :] = value
        packed[pl.ds(at, PAD), :] = value.astype(BF16)
        return carry

    lax.fori_loop(0, channels // PAD, finish, 0, unroll=2)
    packed[channels:, :] = stacked_rows(mean)


def shift_scratch(width):
    return [pltpu.VMEM((2 * width, KS * width), BF16)]


def forward_conv(around, kernel):
    rows, channels, width = around[0].shape
    pixels = rows * width
    return pl.pallas_call(
        forward_conv_kernel,
        out_shape=(
            shape((channels + PAD, pixels), BF16),
            shape((channels, pixels), F32),
            shape((8, pixels), F32),
        ),
        in_specs=[whole] * 7,
        out_specs=(whole,) * 3,
        scratch_shapes=shift_scratch(width),
        compiler_params=params(32),
        cost_estimate=LIGHT,
        name="conv_forward",
    )(*around, kernel)


def backward_conv_kernel(block, above, below, side, above_side, below_side, kernel, cotangent, result, shifts):
    refs = (block, above, below, side, above_side, below_side)
    rows, channels, width = block.shape
    fill_shifts(shifts)

    def step(index, carry):
        at = pl.multiple_of(index * PAD, PAD)
        sums = convolve(refs, shifts, kernel[pl.ds(at, PAD), :], at, PAD, True)
        for k in range(rows):
            result[k, pl.ds(at, PAD)] = (sums[k] + cotangent[k, pl.ds(at, PAD)].astype(F32)).astype(BF16)
        return carry

    lax.fori_loop(0, channels // PAD, step, 0, unroll=2)


def backward_conv(around, kernel, cotangent):
    return pl.pallas_call(
        backward_conv_kernel,
        out_shape=shape(cotangent.shape, BF16),
        in_specs=[whole] * 8,
        out_specs=whole,
        scratch_shapes=shift_scratch(cotangent.shape[2]),
        compiler_params=params(32),
        cost_estimate=LIGHT,
        name="conv_backward",
    )(*around, kernel, cotangent)


def kernel_gradient_kernel(block, above, below, side, above_side, below_side, gradient, result, shifts):
    refs = (block, above, below, side, above_side, below_side)
    rows, channels, width = block.shape
    fill_shifts(shifts)

    def step(index, carry):
        at = pl.multiple_of(index * PAD, PAD)
        moved = shifted_rows(refs, shifts, at, PAD)
        lane = lax.broadcasted_iota(jnp.int32, (PAD, width), 1)
        grads = [gradient[k, pl.ds(at, PAD)].astype(F32) for k in range(rows)]
        sums = jnp.zeros((PAD, width), F32)
        for tap_col in range(KS):
            near = [
                moved[k * PAD : (k + 1) * PAD, tap_col * width : (tap_col + 1) * width]
                for k in range(rows + KS - 1)
            ]
            for tap_row in range(KS):
                total = grads[0] * near[tap_row]
                for k in range(1, rows):
                    total = total + grads[k] * near[k + tap_row]
                tap = tap_row * KS + tap_col
                sums = jnp.where(lane == tap, jnp.sum(total, axis=1, keepdims=True), sums)
        result[pl.ds(at, PAD), :] = sums
        return carry

    lax.fori_loop(0, channels // PAD, step, 0, unroll=2)


def kernel_gradient(around, gradient):
    rows, channels, width = gradient.shape
    return pl.pallas_call(
        kernel_gradient_kernel,
        out_shape=shape((channels, width), F32),
        in_specs=[whole] * 7,
        out_specs=whole,
        scratch_shapes=shift_scratch(width),
        compiler_params=params(32),
        cost_estimate=LIGHT,
        name="kernel_gradient",
    )(*around, gradient)


def pack_kernel(cotangent, scale, gain, packed, gain_rows):
    rows, channels, width = cotangent.shape
    ones = jnp.ones((PAD, width), BF16)
    wide = dot(stacked_rows(scale[...].reshape(1, channels)), ones, COLS_BY_COLS)
    for k in range(rows):
        packed[:, k * width : (k + 1) * width] = (cotangent[k].astype(F32) * wide).astype(BF16)
    gain_rows[...] = stacked_rows(gain[...].reshape(1, channels))


def pack_cotangent(cotangent, scale, gain):
    rows, channels, width = cotangent.shape
    return pl.pallas_call(
        pack_kernel,
        out_shape=(shape((channels, rows * width), BF16), shape((PAD, channels), BF16)),
        in_specs=[whole] * 3,
        out_specs=(whole, whole),
        compiler_params=params(32),
        cost_estimate=LIGHT,
        name="pack_cotangent",
    )(cotangent, scale, gain)


def gelu_parts(values):
    cdf = 0.5 * (1.0 + lax.erf(values * 0.7071067811865476))
    slope = cdf + values * jnp.exp(-0.5 * values * values) * 0.3989422804014327
    return values * cdf, slope


ROWS_BY_COLS = (((1,), (0,)), ((), ()))
COLS_BY_COLS = (((0,), (0,)), ((), ()))
ROWS_BY_ROWS = (((1,), (1,)), ((), ()))


def dot(left, right, dims):
    return lax.dot_general(left, right, dims, preferred_element_type=F32)


def tile_of(hidden_units):
    for size in (256, 128):
        if hidden_units % size == 0:
            return size
    return hidden_units


def fixed(dims):
    return pl.BlockSpec(dims, lambda t: (0,) * len(dims))


def rows_of(tile, width, first=0):
    return pl.BlockSpec((tile, width), lambda t: (t + first, 0))


def columns_of(height, tile, first=0):
    return pl.BlockSpec((height, tile), lambda t: (0, t + first))


def rotated(block):
    count = lax.axis_size("chan")
    return [block] + [
        lax.ppermute(block, "chan", [(i, (i + k) % count) for i in range(count)])
        for k in range(1, count)
    ]


def cot_kernel(cot_all, w_reduce, bias, *refs):
    shares, (gain, wide_bias, back, matrix) = refs[:-4], refs[-4:]
    count, channels, _ = cot_all.shape

    @pl.when(pl.program_id(0) == 0)
    def _():
        ones = jnp.ones((PAD, gain.shape[1]), BF16)
        wide_bias[...] = dot(stacked_rows(bias[...]), ones, COLS_BY_COLS)
        unpack(cot_all, matrix)
        for k in range(count):
            if len(shares) == 1:
                place, share = k, shares[0][k]
            else:
                place, share = lax.rem(lax.axis_index("chan") + count - k, count), shares[k][...]
            at = pl.multiple_of(place * channels, PAD)
            gain[pl.ds(at, channels), :] = dot(share, ones, COLS_BY_COLS)

    back[...] = dot(w_reduce[...], matrix[...], COLS_BY_COLS)


def cot_stage(cot_all, w_reduce, bias, shares):
    pixels = cot_all.shape[2]
    every, units = w_reduce.shape
    tile = tile_of(units)
    return pl.pallas_call(
        cot_kernel,
        grid=(units // tile,),
        out_shape=(shape((every, 128), F32), shape((units, 128), F32), shape((units, pixels), F32)),
        in_specs=[fixed(cot_all.shape), columns_of(every, tile), fixed((1, units))]
        + [fixed(share.shape) for share in shares],
        out_specs=(fixed((every, 128)), fixed((units, 128)), rows_of(tile, pixels)),
        scratch_shapes=[pltpu.VMEM((every, pixels), BF16)],
        compiler_params=params(60),
        cost_estimate=LIGHT,
        name="cotangent_stage",
    )(cot_all, w_reduce, bias[None, :], *shares)


def widened(values, pixels):
    return jnp.concatenate([values] * (pixels // values.shape[1]), axis=1)


def normalise(conv_all, gain, normed):
    count, padded, pixels = conv_all.shape
    channels = padded - PAD
    every = count * channels
    means = [jnp.sum(conv_all[k, channels:, :].astype(F32), axis=0, keepdims=True) for k in range(count)]
    mean = means[0]
    for k in range(1, count):
        mean = mean + means[k]
    mean = mean / count
    squares = jnp.zeros((8, pixels), F32)
    for k in range(count):
        moved = means[k] - mean

        def gather(index, total):
            at = pl.multiple_of(index * PAD, PAD)
            value = conv_all[k, pl.ds(at, PAD), :].astype(F32) + moved
            value = value * value
            return total + value[:8] + value[8:]

        squares = lax.fori_loop(0, channels // PAD, gather, squares, unroll=2)
    deviation = lax.rsqrt(jnp.sum(squares, axis=0, keepdims=True) / every + EPSILON)
    for k in range(count):
        moved = means[k] - mean

        def write(index, carry):
            at = pl.multiple_of(index * PAD, PAD)
            to = pl.multiple_of(k * channels + at, PAD)
            value = (conv_all[k, pl.ds(at, PAD), :].astype(F32) + moved) * deviation
            scale = gain[pl.ds(to, PAD), :]
            for p in range(pixels // 128):
                cut = slice(p * 128, (p + 1) * 128)
                normed[pl.ds(to, PAD), cut] = (value[:, cut] * scale).astype(BF16)
            return carry

        lax.fori_loop(0, channels // PAD, write, 0, unroll=2)
    return mean, deviation


def norm_kernel(conv_all, gain, normed, stats):
    mean, deviation = normalise(conv_all, gain, normed)
    row = lax.broadcasted_iota(jnp.int32, stats.shape, 0)
    stats[...] = jnp.where(row == 0, mean, jnp.where(row == 1, deviation, 0.0))


def norm_stage(conv_all, gain):
    pixels = conv_all.shape[2]
    return pl.pallas_call(
        norm_kernel,
        out_shape=(shape((gain.shape[0], pixels), BF16), shape((8, pixels), F32)),
        in_specs=[whole] * 2,
        out_specs=(whole, whole),
        compiler_params=params(32),
        cost_estimate=LIGHT,
        name="norm",
    )(conv_all, gain)


def block_kernel(steps, normed, gain, w_expand, bias, back, hidden, grad_pre, *refs):
    blocks, normed_sum = refs[:-1], refs[-1]
    at = pl.program_id(0)

    @pl.when(at == 0)
    def _():
        normed_sum[...] = jnp.zeros_like(normed_sum)

    pre = dot(w_expand[...], normed[...], ROWS_BY_COLS) + widened(bias[...], normed.shape[1])
    active, slope = gelu_parts(pre)
    hidden[...] = active.astype(BF16)
    grad = (back[...] * slope).astype(BF16)
    grad_pre[...] = grad
    normed_sum[...] += dot(w_expand[...], grad, COLS_BY_COLS)

    @pl.when(at == steps - 1)
    def _():
        every, pixels = normed.shape
        def step(index, totals):
            cut = pl.ds(pl.multiple_of(index * PAD, PAD), PAD)
            value = normed_sum[cut, :]
            first = value * widened(gain[cut, :], pixels)
            cross = value * normed[cut, :].astype(F32)
            return totals[0] + first[:8] + first[8:], totals[1] + cross[:8] + cross[8:]

        totals = lax.fori_loop(0, every // PAD, step, (jnp.zeros((8, pixels), F32),) * 2, unroll=2)
        moments = stacked_rows(*[jnp.sum(total, axis=0, keepdims=True) for total in totals])
        for k, block in enumerate(blocks):
            height = block.shape[0] - PAD
            place = lax.rem(lax.axis_index("chan") + k, len(blocks)) if len(blocks) > 1 else 0
            block[:height, :] = normed_sum[pl.ds(pl.multiple_of(place * height, PAD), height), :].astype(BF16)
            block[height:, :] = moments


def block_stage(normed, gain, w_expand, bias, back):
    count = lax.axis_size("chan")
    units, every = w_expand.shape
    pixels = normed.shape[1]
    tile = 512 if units % 512 == 0 else tile_of(units)
    steps = units // tile
    blocks = count if count <= 4 else 1
    return pl.pallas_call(
        functools.partial(block_kernel, steps),
        grid=(steps,),
        out_shape=(shape((units, pixels), BF16),) * 2
        + (shape((every // blocks + PAD, pixels), BF16),) * blocks,
        in_specs=[
            fixed(normed.shape),
            fixed(gain.shape),
            rows_of(tile, every),
            rows_of(tile, 128),
            rows_of(tile, pixels),
        ],
        out_specs=(rows_of(tile, pixels),) * 2 + (fixed((every // blocks + PAD, pixels)),) * blocks,
        scratch_shapes=[pltpu.VMEM((every, pixels), F32)],
        compiler_params=params(60),
        cost_estimate=LIGHT,
        name="pointwise_block",
    )(normed, gain, w_expand, bias, back)


def reduced_kernel(weight, hidden, result):
    result[...] = dot(weight[...], hidden[...], ROWS_BY_COLS).astype(BF16)


def reduce_product(w_reduce, hidden):
    every, units = w_reduce.shape
    pixels = hidden.shape[1]
    tile = 512 if every % 512 == 0 else tile_of(every)
    return pl.pallas_call(
        reduced_kernel,
        grid=(every // tile,),
        out_shape=shape((every, pixels), BF16),
        in_specs=[rows_of(tile, units), fixed(hidden.shape)],
        out_specs=rows_of(tile, pixels),
        compiler_params=params(60),
        cost_estimate=LIGHT,
        name="reduced_product",
    )(w_reduce, hidden)


def unpack(cot_all, target):
    channels = cot_all.shape[1]
    for k in range(cot_all.shape[0]):
        target[k * channels : (k + 1) * channels, :] = cot_all[k]


def own_tile_kernel(normed, cot_all, hidden, grad_pre, grad_reduce, grad_expand, cot):
    @pl.when(pl.program_id(0) == 0)
    def _():
        unpack(cot_all, cot)

    grad_reduce[...] = dot(cot[...], hidden[...], ROWS_BY_ROWS).astype(BF16)
    grad_expand[...] = dot(grad_pre[...], normed[...], ROWS_BY_ROWS).astype(BF16)


def own_tile_gradients(normed, cot_all, hidden, grad_pre):
    every, pixels = normed.shape
    units = hidden.shape[0]
    tile = tile_of(units)
    return pl.pallas_call(
        own_tile_kernel,
        grid=(units // tile,),
        out_shape=(shape((every, units), BF16), shape((units, every), BF16)),
        in_specs=[fixed(normed.shape), fixed(cot_all.shape), rows_of(tile, pixels), rows_of(tile, pixels)],
        out_specs=(columns_of(every, tile), rows_of(tile, every)),
        scratch_shapes=[pltpu.VMEM((every, pixels), BF16)],
        compiler_params=params(60),
        cost_estimate=LIGHT,
        name="own_tile_gradients",
    )(normed, cot_all, hidden, grad_pre)


def plus(first, product):
    return (first.astype(F32) + product.astype(BF16).astype(F32)).astype(BF16)


def other_tile_kernel(
    normed, cot_all, reduce_own, expand_own, w_expand, bias, w_reduce, grad_reduce, grad_expand, cot
):
    @pl.when(pl.program_id(0) == 0)
    def _():
        unpack(cot_all, cot)

    pre = dot(w_expand[...], normed[...], ROWS_BY_COLS) + widened(bias[...], normed.shape[1])
    back = dot(w_reduce[...], cot[...], COLS_BY_COLS)
    active, slope = gelu_parts(pre)
    grad_pre = (back * slope).astype(BF16)
    grad_reduce[...] = plus(reduce_own[...], dot(cot[...], active.astype(BF16), ROWS_BY_ROWS))
    grad_expand[...] = plus(expand_own[...], dot(grad_pre, normed[...], ROWS_BY_ROWS))


def two_tile_gradients(normed, cot_all, reduce_own, expand_own, w_expand, bias, w_reduce):
    every, pixels = normed.shape
    units = w_expand.shape[0]
    tile = tile_of(units)
    return pl.pallas_call(
        other_tile_kernel,
        grid=(units // tile,),
        out_shape=(shape((every, units), BF16), shape((units, every), BF16)),
        in_specs=[
            fixed(normed.shape),
            fixed(cot_all.shape),
            columns_of(every, tile),
            rows_of(tile, every),
            rows_of(tile, every),
            rows_of(tile, 128),
            columns_of(every, tile),
        ],
        out_specs=(columns_of(every, tile), rows_of(tile, every)),
        scratch_shapes=[pltpu.VMEM((every, pixels), BF16)],
        compiler_params=params(60),
        cost_estimate=LIGHT,
        name="two_tile_gradients",
    )(normed, cot_all, reduce_own, expand_own, w_expand, bias, w_reduce)


def pair_sum(mine, theirs):
    return (mine.astype(F32) + theirs.astype(F32)).astype(BF16)


def norm_gradient_kernel(every, centered, local, stats, gain, *refs):
    blocks, result = refs[:-1], refs[-1]
    rows, channels, width = result.shape
    mean, deviation = stats[0:1, :], stats[1:2, :]
    first = cross = 0.0
    for block in blocks:
        tail = block[channels:, :]
        first = first + unstacked(tail, 0)
        cross = cross + unstacked(tail, 1)
    first, cross = first / every, cross / every
    shift = local[0:1, :] - mean
    own = lax.axis_index("chan") * channels

    def step(index, carry):
        at = pl.multiple_of(index * PAD, PAD)
        cut = pl.ds(at, PAD)
        hat = (centered[cut, :] + shift) * deviation
        value = blocks[0][cut, :].astype(F32)
        for block in blocks[1:]:
            value = value + block[cut, :].astype(F32)
        value = value * widened(gain[pl.ds(pl.multiple_of(own + at, PAD), PAD), :], value.shape[1])
        value = ((value - first - hat * cross) * deviation).astype(BF16)
        for k in range(rows):
            result[k, cut] = value[:, k * width : (k + 1) * width]
        return carry

    lax.fori_loop(0, channels // PAD, step, 0)


def norm_gradient(every, dims, blocks, centered, local, stats, gain):
    return pl.pallas_call(
        functools.partial(norm_gradient_kernel, every),
        out_shape=shape(dims, BF16),
        in_specs=[whole] * (4 + len(blocks)),
        out_specs=whole,
        compiler_params=params(32),
        cost_estimate=LIGHT,
        name="norm_gradient",
    )(centered, local, stats, gain, *blocks)


def scattered(blocks):
    count = lax.axis_size("chan")
    if len(blocks) == 1:
        height = blocks[0].shape[0] - PAD
        total = lax.psum_scatter(blocks[0][:height], "chan", scatter_dimension=0, tiled=True)
        tail = blocks[0][height:].astype(F32)
        sums = jnp.stack([jnp.sum(tail[:3], axis=0), jnp.sum(tail[3:6], axis=0)])
        sums = lax.psum(sums, "chan")
        parts = [part for row in sums for part in pieces(row)]
        tail = jnp.zeros(tail.shape, BF16).at[:6].set(jnp.stack(parts))
        return [jnp.concatenate([total, tail])]
    return [blocks[0]] + [
        lax.ppermute(blocks[k], "chan", [(i, (i + k) % count) for i in range(count)])
        for k in range(1, count)
    ]


def after(values, *others):
    return lax.optimization_barrier((values, others))[0]


def swap(values, axis):
    return lax.ppermute(values, axis, [(0, 1), (1, 0)])


def on_device(
    image, kernel, layer_norm_weight, w_expand, bias_expand, w_reduce, layer_scale, cotangent
):
    channels, tile_rows, tile_cols = image.shape
    pixels = tile_rows * tile_cols
    every = w_reduce.shape[0]
    two_tiles = lax.axis_size("rows") == 2 and lax.axis_size("cols") == 2

    image_rows = jnp.transpose(image, (1, 0, 2))
    around = surroundings(image_rows)
    cot_rows = jnp.transpose(cotangent, (1, 0, 2))
    packed_cot, gain_rows = pack_cotangent(cot_rows, layer_scale, layer_norm_weight)
    cot_all = lax.all_gather(packed_cot, "chan")

    packed_conv, centered, local = forward_conv(around, kernel)
    conv_all = lax.all_gather(packed_conv, "chan")
    cot_all, bias = after((cot_all, bias_expand), packed_conv)
    gain_rows = after(gain_rows, packed_conv)
    count = lax.axis_size("chan")
    shares = [lax.all_gather(gain_rows, "chan")]
    if count <= 4:
        turns = [[(i, (i + k) % count) for i in range(count)] for k in range(1, count)]
        shares = [gain_rows] + [lax.ppermute(gain_rows, "chan", turn) for turn in turns]
    gain, bias, back = cot_stage(cot_all, w_reduce, bias, shares)
    normed, stats = norm_stage(conv_all, gain)
    ready = normed
    if two_tiles:
        cot_other = swap(cot_all, "rows")
        normed_other = swap(normed, "rows")
        ready = after(normed, cot_other)
    hidden, grad_pre, *blocks = block_stage(ready, gain, w_expand, bias, back)
    norm_inputs = (scattered(blocks), centered, local, stats)
    product = reduce_product(w_reduce, hidden)
    reduced = lax.psum_scatter(product, "chan", scatter_dimension=0, tiled=True)

    if two_tiles:
        own = own_tile_gradients(normed, cot_all, after(hidden, product), grad_pre)
        found = two_tile_gradients(normed_other, cot_other, *own, w_expand, bias, w_reduce)
        norm_inputs = after(norm_inputs, found)
    gradient = norm_gradient(every, image_rows.shape, *norm_inputs, gain)
    taps = kernel_gradient(around, gradient)
    grad_around = surroundings(gradient, taps if two_tiles else None)
    if two_tiles:
        theirs = [swap(after(mine, gradient), "cols") for mine in found]
        grad_reduce = pair_sum(found[0], theirs[0])
        grad_around = after(grad_around, grad_reduce)
    grad_rows = backward_conv(grad_around, kernel, cot_rows)
    grad_input = jnp.transpose(grad_rows, (1, 0, 2))
    if two_tiles:
        taps = after(taps, grad_rows)
        taps = taps + swap(taps, "cols")
        taps = taps + swap(taps, "rows")
        grad_expand = pair_sum(found[1], theirs[1])
        reduced = after(reduced, grad_expand, taps)
    else:
        taps = lax.psum(taps, ("rows", "cols"))
        cot = cot_all[:, :channels, :].reshape(every, pixels)
        grad_reduce = dot(cot, hidden, ROWS_BY_ROWS).astype(BF16)
        grad_expand = dot(grad_pre, normed, ROWS_BY_ROWS).astype(BF16)
        grad_reduce, grad_expand = lax.psum((grad_reduce, grad_expand), ("rows", "cols"))
    taps = taps[:, : KS * KS]

    output = (
        image.reshape(channels, pixels).astype(F32) + layer_scale[:, None] * reduced.astype(F32)
    ).astype(BF16).reshape(image.shape)
    return output, grad_input, grad_expand, grad_reduce, taps


def solution(mesh):
    placed = (
        P("chan", ("groups", "rows"), "cols"),
        P("chan", None),
        P("chan"),
        P("chan", None),
        P("chan"),
        P(None, "chan"),
        P("chan"),
        P("chan", ("groups", "rows"), "cols"),
    )
    return jax.shard_map(
        on_device,
        mesh=mesh,
        in_specs=placed,
        out_specs=(
            P("chan", ("groups", "rows"), "cols"),
            P("chan", ("groups", "rows"), "cols"),
            P(("groups", "chan"), None),
            P("groups", "chan"),
            P(("groups", "chan"), None),
        ),
        check_vma=False,
    )
```

```python
import functools

import jax
import jax.numpy as jnp
from jax import lax
from jax.experimental import pallas as pl
from jax.experimental.pallas import tpu as pltpu
from jax.sharding import PartitionSpec as P

KS = 7
HALF = KS // 2
PAD = 16
EPSILON = 1e-06
MIB = 1024 * 1024
F32 = jnp.float32
BF16 = jnp.bfloat16

whole = pl.BlockSpec(memory_space=pltpu.VMEM)
anywhere = pl.BlockSpec(memory_space=pl.ANY)
LIGHT = pl.CostEstimate(flops=1000, bytes_accessed=1000, transcendentals=0)


def params(mib):
    return pltpu.CompilerParams(vmem_limit_bytes=mib * MIB)


def shape(dims, dtype):
    return jax.ShapeDtypeStruct(dims, dtype)


def pieces(values):
    high = values.astype(BF16)
    rest = values - high.astype(F32)
    middle = rest.astype(BF16)
    low = (rest - middle.astype(F32)).astype(BF16)
    return high, middle, low


def stacked_rows(*rows):
    width = rows[0].shape[1]
    row = lax.broadcasted_iota(jnp.int32, (PAD, width), 0)
    block = jnp.zeros((PAD, width), F32)
    for first, values in enumerate(rows):
        for index, part in enumerate(pieces(values)):
            block = jnp.where(row == 3 * first + index, part.astype(F32), block)
    return block.astype(BF16)


def unstacked(block, first):
    return jnp.sum(block.astype(F32)[3 * first : 3 * first + 3, :], axis=0, keepdims=True)


def from_sides(low_source, high_source, axis):
    count = lax.axis_size(axis)
    if count == 2:
        index = lax.axis_index(axis)
        sent = jnp.where(index == 0, low_source, high_source)
        got = lax.ppermute(sent, axis, [(0, 1), (1, 0)])
        return got, got
    forward = [(i, i + 1) for i in range(count - 1)]
    backward = [(i + 1, i) for i in range(count - 1)]
    return lax.ppermute(low_source, axis, forward), lax.ppermute(high_source, axis, backward)


def edges(block, axis):
    count = lax.axis_size(axis)
    if count == 2:
        return lax.ppermute(block, axis, [(0, 1), (1, 0)])
    low, high = from_sides(block, block, axis)
    width = block.shape[-1]
    lane = lax.broadcasted_iota(jnp.int32, block.shape, block.ndim - 1)
    return jnp.where(lane < width // 2, high, low)


def surroundings(block, before_corner=None):
    rows = block.shape[0]
    above, below = from_sides(block[rows - HALF :], block[:HALF], "rows")
    side = edges(block, "cols")
    if before_corner is not None:
        above, below = after((above, below), before_corner)
    if lax.axis_size("rows") == 2:
        corner = edges(above, "cols")
        return block, above, below, side, corner, corner
    return block, above, below, side, edges(above, "cols"), edges(below, "cols")


def flag(test):
    return jnp.where(test, 1.0, 0.0).astype(F32)


def fill_shifts(shifts):
    width = shifts.shape[0] // 2
    col = lax.axis_index("cols")
    has_right, has_left = flag(col < lax.axis_size("cols") - 1), flag(col > 0)
    source = lax.broadcasted_iota(jnp.int32, (width, width), 0)
    target = lax.broadcasted_iota(jnp.int32, (width, width), 1)
    for tap in range(KS):
        cut = slice(tap * width, (tap + 1) * width)
        wanted = target + (tap - HALF)
        shifts[:width, cut] = jnp.where(source == wanted, 1.0, 0.0).astype(BF16)
        right = jnp.where(source + width == wanted, has_right, 0.0)
        left = jnp.where(source - width == wanted, has_left, 0.0)
        shifts[width:, cut] = (right + left).astype(BF16)


def shifted_rows(refs, shifts, at, count):
    block, above, below, side, above_side, below_side = refs
    row = lax.axis_index("rows")
    has_above = flag(row > 0).astype(BF16)
    has_below = flag(row < lax.axis_size("rows") - 1).astype(BF16)
    rows = block.shape[0]
    cut = pl.ds(at, count)
    found = [jnp.concatenate([above[k, cut], above_side[k, cut]], axis=1) * has_above for k in range(HALF)]
    found += [jnp.concatenate([block[k, cut], side[k, cut]], axis=1) for k in range(rows)]
    found += [jnp.concatenate([below[k, cut], below_side[k, cut]], axis=1) * has_below for k in range(HALF)]
    return dot(jnp.concatenate(found, axis=0), shifts[...], ROWS_BY_COLS)


def convolve(refs, shifts, taps, at, count, flipped):
    rows, _, width = refs[0].shape
    moved = shifted_rows(refs, shifts, at, count)
    sums = [None] * rows
    for tap_col in range(KS):
        near = [
            moved[k * count : (k + 1) * count, tap_col * width : (tap_col + 1) * width]
            for k in range(rows + KS - 1)
        ]
        for tap_row in range(KS):
            tap = tap_row * KS + tap_col
            tap = KS * KS - 1 - tap if flipped else tap
            weight = jnp.broadcast_to(taps[:, tap : tap + 1], (count, width))
            for k in range(rows):
                term = weight * near[k + tap_row]
                sums[k] = term if sums[k] is None else sums[k] + term
    return sums


def forward_conv_kernel(block, above, below, side, above_side, below_side, kernel, packed, centered, local, shifts):
    refs = (block, above, below, side, above_side, below_side)
    rows, channels, width = block.shape
    fill_shifts(shifts)

    def step(index, totals):
        at = pl.multiple_of(index * PAD, PAD)
        sums = convolve(refs, shifts, kernel[pl.ds(at, PAD), :], at, PAD, False)
        for k in range(rows):
            centered[pl.ds(at, PAD), k * width : (k + 1) * width] = sums[k]
        return tuple(total + value[:8] + value[8:] for total, value in zip(totals, sums))

    totals = lax.fori_loop(
        0, channels // PAD, step, tuple(jnp.zeros((8, width), F32) for _ in range(rows)), unroll=2
    )
    mean = jnp.concatenate([jnp.sum(total, axis=0, keepdims=True) for total in totals], axis=1) / channels
    local[...] = jnp.broadcast_to(mean, local.shape)

    def finish(index, carry):
        at = pl.multiple_of(index * PAD, PAD)
        value = centered[pl.ds(at, PAD), :] - mean
        centered[pl.ds(at, PAD), :] = value
        packed[pl.ds(at, PAD), :] = value.astype(BF16)
        return carry

    lax.fori_loop(0, channels // PAD, finish, 0, unroll=2)
    packed[channels:, :] = stacked_rows(mean)


def shift_scratch(width):
    return [pltpu.VMEM((2 * width, KS * width), BF16)]


def forward_conv(around, kernel):
    rows, channels, width = around[0].shape
    pixels = rows * width
    return pl.pallas_call(
        forward_conv_kernel,
        out_shape=(
            shape((channels + PAD, pixels), BF16),
            shape((channels, pixels), F32),
            shape((8, pixels), F32),
        ),
        in_specs=[whole] * 7,
        out_specs=(whole,) * 3,
        scratch_shapes=shift_scratch(width),
        compiler_params=params(32),
        cost_estimate=LIGHT,
        name="conv_forward",
    )(*around, kernel)


def backward_conv_kernel(block, above, below, side, above_side, below_side, kernel, cotangent, result, shifts):
    refs = (block, above, below, side, above_side, below_side)
    rows, channels, width = block.shape
    fill_shifts(shifts)

    def step(index, carry):
        at = pl.multiple_of(index * PAD, PAD)
        sums = convolve(refs, shifts, kernel[pl.ds(at, PAD), :], at, PAD, True)
        for k in range(rows):
            result[k, pl.ds(at, PAD)] = (sums[k] + cotangent[k, pl.ds(at, PAD)].astype(F32)).astype(BF16)
        return carry

    lax.fori_loop(0, channels // PAD, step, 0, unroll=2)


def backward_conv(around, kernel, cotangent):
    return pl.pallas_call(
        backward_conv_kernel,
        out_shape=shape(cotangent.shape, BF16),
        in_specs=[whole] * 8,
        out_specs=whole,
        scratch_shapes=shift_scratch(cotangent.shape[2]),
        compiler_params=params(32),
        cost_estimate=LIGHT,
        name="conv_backward",
    )(*around, kernel, cotangent)


def kernel_gradient_kernel(block, above, below, side, above_side, below_side, gradient, result, shifts):
    refs = (block, above, below, side, above_side, below_side)
    rows, channels, width = block.shape
    fill_shifts(shifts)

    def step(index, carry):
        at = pl.multiple_of(index * PAD, PAD)
        moved = shifted_rows(refs, shifts, at, PAD)
        lane = lax.broadcasted_iota(jnp.int32, (PAD, width), 1)
        grads = [gradient[k, pl.ds(at, PAD)].astype(F32) for k in range(rows)]
        sums = jnp.zeros((PAD, width), F32)
        for tap_col in range(KS):
            near = [
                moved[k * PAD : (k + 1) * PAD, tap_col * width : (tap_col + 1) * width]
                for k in range(rows + KS - 1)
            ]
            for tap_row in range(KS):
                total = grads[0] * near[tap_row]
                for k in range(1, rows):
                    total = total + grads[k] * near[k + tap_row]
                tap = tap_row * KS + tap_col
                sums = jnp.where(lane == tap, jnp.sum(total, axis=1, keepdims=True), sums)
        result[pl.ds(at, PAD), :] = sums
        return carry

    lax.fori_loop(0, channels // PAD, step, 0, unroll=2)


def kernel_gradient(around, gradient):
    rows, channels, width = gradient.shape
    return pl.pallas_call(
        kernel_gradient_kernel,
        out_shape=shape((channels, width), F32),
        in_specs=[whole] * 7,
        out_specs=whole,
        scratch_shapes=shift_scratch(width),
        compiler_params=params(32),
        cost_estimate=LIGHT,
        name="kernel_gradient",
    )(*around, gradient)


def pack_kernel(cotangent, scale, gain, packed, gain_rows):
    rows, channels, width = cotangent.shape
    ones = jnp.ones((PAD, width), BF16)
    wide = dot(stacked_rows(scale[...].reshape(1, channels)), ones, COLS_BY_COLS)
    for k in range(rows):
        packed[:, k * width : (k + 1) * width] = (cotangent[k].astype(F32) * wide).astype(BF16)
    gain_rows[...] = stacked_rows(gain[...].reshape(1, channels))


def pack_cotangent(cotangent, scale, gain):
    rows, channels, width = cotangent.shape
    return pl.pallas_call(
        pack_kernel,
        out_shape=(shape((channels, rows * width), BF16), shape((PAD, channels), BF16)),
        in_specs=[whole] * 3,
        out_specs=(whole, whole),
        compiler_params=params(32),
        cost_estimate=LIGHT,
        name="pack_cotangent",
    )(cotangent, scale, gain)


def gelu_parts(values):
    cdf = 0.5 * (1.0 + lax.erf(values * 0.7071067811865476))
    slope = cdf + values * jnp.exp(-0.5 * values * values) * 0.3989422804014327
    return values * cdf, slope


ROWS_BY_COLS = (((1,), (0,)), ((), ()))
COLS_BY_COLS = (((0,), (0,)), ((), ()))
ROWS_BY_ROWS = (((1,), (1,)), ((), ()))


def dot(left, right, dims):
    return lax.dot_general(left, right, dims, preferred_element_type=F32)


def tile_of(hidden_units):
    for size in (256, 128):
        if hidden_units % size == 0:
            return size
    return hidden_units


def fixed(dims):
    return pl.BlockSpec(dims, lambda t: (0,) * len(dims))


def rows_of(tile, width, first=0):
    return pl.BlockSpec((tile, width), lambda t: (t + first, 0))


def columns_of(height, tile, first=0):
    return pl.BlockSpec((height, tile), lambda t: (0, t + first))


def rotated(block):
    count = lax.axis_size("chan")
    return [block] + [
        lax.ppermute(block, "chan", [(i, (i + k) % count) for i in range(count)])
        for k in range(1, count)
    ]


def cot_kernel(cot_all, w_reduce, bias, *refs):
    shares, (gain, wide_bias, back, matrix) = refs[:-4], refs[-4:]
    count, channels, _ = cot_all.shape

    @pl.when(pl.program_id(0) == 0)
    def _():
        ones = jnp.ones((PAD, gain.shape[1]), BF16)
        wide_bias[...] = dot(stacked_rows(bias[...]), ones, COLS_BY_COLS)
        unpack(cot_all, matrix)
        for k in range(count):
            if len(shares) == 1:
                place, share = k, shares[0][k]
            else:
                place, share = lax.rem(lax.axis_index("chan") + count - k, count), shares[k][...]
            at = pl.multiple_of(place * channels, PAD)
            gain[pl.ds(at, channels), :] = dot(share, ones, COLS_BY_COLS)

    back[...] = dot(w_reduce[...], matrix[...], COLS_BY_COLS)


def cot_stage(cot_all, w_reduce, bias, shares):
    pixels = cot_all.shape[2]
    every, units = w_reduce.shape
    tile = tile_of(units)
    return pl.pallas_call(
        cot_kernel,
        grid=(units // tile,),
        out_shape=(shape((every, 128), F32), shape((units, 128), F32), shape((units, pixels), F32)),
        in_specs=[fixed(cot_all.shape), columns_of(every, tile), fixed((1, units))]
        + [fixed(share.shape) for share in shares],
        out_specs=(fixed((every, 128)), fixed((units, 128)), rows_of(tile, pixels)),
        scratch_shapes=[pltpu.VMEM((every, pixels), BF16)],
        compiler_params=params(60),
        cost_estimate=LIGHT,
        name="cotangent_stage",
    )(cot_all, w_reduce, bias[None, :], *shares)


def widened(values, pixels):
    return jnp.concatenate([values] * (pixels // values.shape[1]), axis=1)


def normalise(conv_all, gain, normed):
    count, padded, pixels = conv_all.shape
    channels = padded - PAD
    every = count * channels
    means = [jnp.sum(conv_all[k, channels:, :].astype(F32), axis=0, keepdims=True) for k in range(count)]
    mean = means[0]
    for k in range(1, count):
        mean = mean + means[k]
    mean = mean / count
    squares = jnp.zeros((8, pixels), F32)
    for k in range(count):
        moved = means[k] - mean

        def gather(index, total):
            at = pl.multiple_of(index * PAD, PAD)
            value = conv_all[k, pl.ds(at, PAD), :].astype(F32) + moved
            value = value * value
            return total + value[:8] + value[8:]

        squares = lax.fori_loop(0, channels // PAD, gather, squares, unroll=2)
    deviation = lax.rsqrt(jnp.sum(squares, axis=0, keepdims=True) / every + EPSILON)
    for k in range(count):
        moved = means[k] - mean

        def write(index, carry):
            at = pl.multiple_of(index * PAD, PAD)
            to = pl.multiple_of(k * channels + at, PAD)
            value = (conv_all[k, pl.ds(at, PAD), :].astype(F32) + moved) * deviation
            scale = gain[pl.ds(to, PAD), :]
            for p in range(pixels // 128):
                cut = slice(p * 128, (p + 1) * 128)
                normed[pl.ds(to, PAD), cut] = (value[:, cut] * scale).astype(BF16)
            return carry

        lax.fori_loop(0, channels // PAD, write, 0, unroll=2)
    return mean, deviation


def norm_kernel(conv_all, gain, normed, stats):
    mean, deviation = normalise(conv_all, gain, normed)
    row = lax.broadcasted_iota(jnp.int32, stats.shape, 0)
    stats[...] = jnp.where(row == 0, mean, jnp.where(row == 1, deviation, 0.0))


def norm_stage(conv_all, gain):
    pixels = conv_all.shape[2]
    return pl.pallas_call(
        norm_kernel,
        out_shape=(shape((gain.shape[0], pixels), BF16), shape((8, pixels), F32)),
        in_specs=[whole] * 2,
        out_specs=(whole, whole),
        compiler_params=params(32),
        cost_estimate=LIGHT,
        name="norm",
    )(conv_all, gain)


def block_kernel(steps, normed, gain, w_expand, bias, back, hidden, grad_pre, *refs):
    blocks, normed_sum = refs[:-1], refs[-1]
    at = pl.program_id(0)

    @pl.when(at == 0)
    def _():
        normed_sum[...] = jnp.zeros_like(normed_sum)

    pre = dot(w_expand[...], normed[...], ROWS_BY_COLS) + widened(bias[...], normed.shape[1])
    active, slope = gelu_parts(pre)
    hidden[...] = active.astype(BF16)
    grad = (back[...] * slope).astype(BF16)
    grad_pre[...] = grad
    normed_sum[...] += dot(w_expand[...], grad, COLS_BY_COLS)

    @pl.when(at == steps - 1)
    def _():
        every, pixels = normed.shape
        def step(index, totals):
            cut = pl.ds(pl.multiple_of(index * PAD, PAD), PAD)
            value = normed_sum[cut, :]
            first = value * widened(gain[cut, :], pixels)
            cross = value * normed[cut, :].astype(F32)
            return totals[0] + first[:8] + first[8:], totals[1] + cross[:8] + cross[8:]

        totals = lax.fori_loop(0, every // PAD, step, (jnp.zeros((8, pixels), F32),) * 2, unroll=2)
        moments = stacked_rows(*[jnp.sum(total, axis=0, keepdims=True) for total in totals])
        for k, block in enumerate(blocks):
            height = block.shape[0] - PAD
            place = lax.rem(lax.axis_index("chan") + k, len(blocks)) if len(blocks) > 1 else 0
            block[:height, :] = normed_sum[pl.ds(pl.multiple_of(place * height, PAD), height), :].astype(BF16)
            block[height:, :] = moments


def block_stage(normed, gain, w_expand, bias, back):
    count = lax.axis_size("chan")
    units, every = w_expand.shape
    pixels = normed.shape[1]
    tile = 512 if units % 512 == 0 else tile_of(units)
    steps = units // tile
    blocks = count if count <= 4 else 1
    return pl.pallas_call(
        functools.partial(block_kernel, steps),
        grid=(steps,),
        out_shape=(shape((units, pixels), BF16),) * 2
        + (shape((every // blocks + PAD, pixels), BF16),) * blocks,
        in_specs=[
            fixed(normed.shape),
            fixed(gain.shape),
            rows_of(tile, every),
            rows_of(tile, 128),
            rows_of(tile, pixels),
        ],
        out_specs=(rows_of(tile, pixels),) * 2 + (fixed((every // blocks + PAD, pixels)),) * blocks,
        scratch_shapes=[pltpu.VMEM((every, pixels), F32)],
        compiler_params=params(60),
        cost_estimate=LIGHT,
        name="pointwise_block",
    )(normed, gain, w_expand, bias, back)


def reduced_kernel(weight, hidden, result):
    result[...] = dot(weight[...], hidden[...], ROWS_BY_COLS).astype(BF16)


def reduce_product(w_reduce, hidden):
    every, units = w_reduce.shape
    pixels = hidden.shape[1]
    tile = 512 if every % 512 == 0 else tile_of(every)
    return pl.pallas_call(
        reduced_kernel,
        grid=(every // tile,),
        out_shape=shape((every, pixels), BF16),
        in_specs=[rows_of(tile, units), fixed(hidden.shape)],
        out_specs=rows_of(tile, pixels),
        compiler_params=params(60),
        cost_estimate=LIGHT,
        name="reduced_product",
    )(w_reduce, hidden)


def unpack(cot_all, target):
    channels = cot_all.shape[1]
    for k in range(cot_all.shape[0]):
        target[k * channels : (k + 1) * channels, :] = cot_all[k]


def own_tile_kernel(normed, cot_all, hidden, grad_pre, grad_reduce, grad_expand, cot):
    @pl.when(pl.program_id(0) == 0)
    def _():
        unpack(cot_all, cot)

    grad_reduce[...] = dot(cot[...], hidden[...], ROWS_BY_ROWS).astype(BF16)
    grad_expand[...] = dot(grad_pre[...], normed[...], ROWS_BY_ROWS).astype(BF16)


def own_tile_gradients(normed, cot_all, hidden, grad_pre):
    every, pixels = normed.shape
    units = hidden.shape[0]
    tile = 512 if units % 512 == 0 else tile_of(units)
    return pl.pallas_call(
        own_tile_kernel,
        grid=(units // tile,),
        out_shape=(shape((every, units), BF16), shape((units, every), BF16)),
        in_specs=[fixed(normed.shape), fixed(cot_all.shape), rows_of(tile, pixels), rows_of(tile, pixels)],
        out_specs=(columns_of(every, tile), rows_of(tile, every)),
        scratch_shapes=[pltpu.VMEM((every, pixels), BF16)],
        compiler_params=params(60),
        cost_estimate=LIGHT,
        name="own_tile_gradients",
    )(normed, cot_all, hidden, grad_pre)


def plus(first, product):
    return (first.astype(F32) + product.astype(BF16).astype(F32)).astype(BF16)


def other_tile_kernel(
    normed, cot_all, reduce_own, expand_own, w_expand, bias, w_reduce, grad_reduce, grad_expand, cot
):
    @pl.when(pl.program_id(0) == 0)
    def _():
        unpack(cot_all, cot)

    pre = dot(w_expand[...], normed[...], ROWS_BY_COLS) + widened(bias[...], normed.shape[1])
    back = dot(w_reduce[...], cot[...], COLS_BY_COLS)
    active, slope = gelu_parts(pre)
    grad_pre = (back * slope).astype(BF16)
    grad_reduce[...] = plus(reduce_own[...], dot(cot[...], active.astype(BF16), ROWS_BY_ROWS))
    grad_expand[...] = plus(expand_own[...], dot(grad_pre, normed[...], ROWS_BY_ROWS))


def two_tile_gradients(normed, cot_all, reduce_own, expand_own, w_expand, bias, w_reduce):
    every, pixels = normed.shape
    units = w_expand.shape[0]
    tile = 384 if units % 384 == 0 else tile_of(units)
    return pl.pallas_call(
        other_tile_kernel,
        grid=(units // tile,),
        out_shape=(shape((every, units), BF16), shape((units, every), BF16)),
        in_specs=[
            fixed(normed.shape),
            fixed(cot_all.shape),
            columns_of(every, tile),
            rows_of(tile, every),
            rows_of(tile, every),
            rows_of(tile, 128),
            columns_of(every, tile),
        ],
        out_specs=(columns_of(every, tile), rows_of(tile, every)),
        scratch_shapes=[pltpu.VMEM((every, pixels), BF16)],
        compiler_params=params(60),
        cost_estimate=LIGHT,
        name="two_tile_gradients",
    )(normed, cot_all, reduce_own, expand_own, w_expand, bias, w_reduce)


def pair_sum(mine, theirs):
    return (mine.astype(F32) + theirs.astype(F32)).astype(BF16)


def norm_gradient_kernel(every, centered, local, stats, gain, *refs):
    blocks, result = refs[:-1], refs[-1]
    rows, channels, width = result.shape
    mean, deviation = stats[0:1, :], stats[1:2, :]
    first = cross = 0.0
    for block in blocks:
        tail = block[channels:, :]
        first = first + unstacked(tail, 0)
        cross = cross + unstacked(tail, 1)
    first, cross = first / every, cross / every
    shift = local[0:1, :] - mean
    own = lax.axis_index("chan") * channels

    def step(index, carry):
        at = pl.multiple_of(index * PAD, PAD)
        cut = pl.ds(at, PAD)
        hat = (centered[cut, :] + shift) * deviation
        value = blocks[0][cut, :].astype(F32)
        for block in blocks[1:]:
            value = value + block[cut, :].astype(F32)
        value = value * widened(gain[pl.ds(pl.multiple_of(own + at, PAD), PAD), :], value.shape[1])
        value = ((value - first - hat * cross) * deviation).astype(BF16)
        for k in range(rows):
            result[k, cut] = value[:, k * width : (k + 1) * width]
        return carry

    lax.fori_loop(0, channels // PAD, step, 0)


def norm_gradient(every, dims, blocks, centered, local, stats, gain):
    return pl.pallas_call(
        functools.partial(norm_gradient_kernel, every),
        out_shape=shape(dims, BF16),
        in_specs=[whole] * (4 + len(blocks)),
        out_specs=whole,
        compiler_params=params(32),
        cost_estimate=LIGHT,
        name="norm_gradient",
    )(centered, local, stats, gain, *blocks)


def scattered(blocks):
    count = lax.axis_size("chan")
    if len(blocks) == 1:
        height = blocks[0].shape[0] - PAD
        total = lax.psum_scatter(blocks[0][:height], "chan", scatter_dimension=0, tiled=True)
        tail = blocks[0][height:].astype(F32)
        sums = jnp.stack([jnp.sum(tail[:3], axis=0), jnp.sum(tail[3:6], axis=0)])
        sums = lax.psum(sums, "chan")
        parts = [part for row in sums for part in pieces(row)]
        tail = jnp.zeros(tail.shape, BF16).at[:6].set(jnp.stack(parts))
        return [jnp.concatenate([total, tail])]
    return [blocks[0]] + [
        lax.ppermute(blocks[k], "chan", [(i, (i + k) % count) for i in range(count)])
        for k in range(1, count)
    ]


def after(values, *others):
    return lax.optimization_barrier((values, others))[0]


def swap(values, axis):
    return lax.ppermute(values, axis, [(0, 1), (1, 0)])


def on_device(
    image, kernel, layer_norm_weight, w_expand, bias_expand, w_reduce, layer_scale, cotangent
):
    channels, tile_rows, tile_cols = image.shape
    pixels = tile_rows * tile_cols
    every = w_reduce.shape[0]
    two_tiles = lax.axis_size("rows") == 2 and lax.axis_size("cols") == 2

    image_rows = jnp.transpose(image, (1, 0, 2))
    around = surroundings(image_rows)
    cot_rows = jnp.transpose(cotangent, (1, 0, 2))
    packed_cot, gain_rows = pack_cotangent(cot_rows, layer_scale, layer_norm_weight)
    cot_all = lax.all_gather(packed_cot, "chan")

    packed_conv, centered, local = forward_conv(around, kernel)
    conv_all = lax.all_gather(packed_conv, "chan")
    cot_all, bias = after((cot_all, bias_expand), packed_conv)
    gain_rows = after(gain_rows, packed_conv)
    count = lax.axis_size("chan")
    shares = [lax.all_gather(gain_rows, "chan")]
    if count <= 4:
        turns = [[(i, (i + k) % count) for i in range(count)] for k in range(1, count)]
        shares = [gain_rows] + [lax.ppermute(gain_rows, "chan", turn) for turn in turns]
    gain, bias, back = cot_stage(cot_all, w_reduce, bias, shares)
    normed, stats = norm_stage(conv_all, gain)
    ready = normed
    if two_tiles:
        cot_other = swap(cot_all, "rows")
        normed_other = swap(normed, "rows")
        ready = after(normed, cot_other)
    hidden, grad_pre, *blocks = block_stage(ready, gain, w_expand, bias, back)
    norm_inputs = (scattered(blocks), centered, local, stats)
    product = reduce_product(w_reduce, hidden)
    reduced = lax.psum_scatter(product, "chan", scatter_dimension=0, tiled=True)

    if two_tiles:
        own = own_tile_gradients(normed, cot_all, after(hidden, product), grad_pre)
        found = two_tile_gradients(normed_other, cot_other, *own, w_expand, bias, w_reduce)
        norm_inputs = after(norm_inputs, found)
    gradient = norm_gradient(every, image_rows.shape, *norm_inputs, gain)
    taps = kernel_gradient(around, gradient)
    grad_around = surroundings(gradient, taps if two_tiles else None)
    if two_tiles:
        theirs = [swap(after(mine, gradient), "cols") for mine in found]
        grad_reduce = pair_sum(found[0], theirs[0])
        grad_around = after(grad_around, grad_reduce)
    grad_rows = backward_conv(grad_around, kernel, cot_rows)
    grad_input = jnp.transpose(grad_rows, (1, 0, 2))
    if two_tiles:
        taps = after(taps, grad_rows)
        taps = taps + swap(taps, "cols")
        taps = taps + swap(taps, "rows")
        grad_expand = pair_sum(found[1], theirs[1])
        reduced = after(reduced, grad_expand, taps)
    else:
        taps = lax.psum(taps, ("rows", "cols"))
        cot = cot_all[:, :channels, :].reshape(every, pixels)
        grad_reduce = dot(cot, hidden, ROWS_BY_ROWS).astype(BF16)
        grad_expand = dot(grad_pre, normed, ROWS_BY_ROWS).astype(BF16)
        grad_reduce, grad_expand = lax.psum((grad_reduce, grad_expand), ("rows", "cols"))
    taps = taps[:, : KS * KS]

    output = (
        image.reshape(channels, pixels).astype(F32) + layer_scale[:, None] * reduced.astype(F32)
    ).astype(BF16).reshape(image.shape)
    return output, grad_input, grad_expand, grad_reduce, taps


def solution(mesh):
    placed = (
        P("chan", ("groups", "rows"), "cols"),
        P("chan", None),
        P("chan"),
        P("chan", None),
        P("chan"),
        P(None, "chan"),
        P("chan"),
        P("chan", ("groups", "rows"), "cols"),
    )
    return jax.shard_map(
        on_device,
        mesh=mesh,
        in_specs=placed,
        out_specs=(
            P("chan", ("groups", "rows"), "cols"),
            P("chan", ("groups", "rows"), "cols"),
            P(("groups", "chan"), None),
            P("groups", "chan"),
            P(("groups", "chan"), None),
        ),
        check_vma=False,
    )
```

```python
import functools

import jax
import jax.numpy as jnp
from jax import lax
from jax.experimental import pallas as pl
from jax.experimental.pallas import tpu as pltpu
from jax.sharding import PartitionSpec as P

KS = 7
HALF = KS // 2
PAD = 16
EPSILON = 1e-06
MIB = 1024 * 1024
F32 = jnp.float32
BF16 = jnp.bfloat16

whole = pl.BlockSpec(memory_space=pltpu.VMEM)
anywhere = pl.BlockSpec(memory_space=pl.ANY)
LIGHT = pl.CostEstimate(flops=1000, bytes_accessed=1000, transcendentals=0)


def params(mib):
    return pltpu.CompilerParams(vmem_limit_bytes=mib * MIB)


def shape(dims, dtype):
    return jax.ShapeDtypeStruct(dims, dtype)


def pieces(values):
    high = values.astype(BF16)
    rest = values - high.astype(F32)
    middle = rest.astype(BF16)
    low = (rest - middle.astype(F32)).astype(BF16)
    return high, middle, low


def stacked_rows(*rows):
    width = rows[0].shape[1]
    row = lax.broadcasted_iota(jnp.int32, (PAD, width), 0)
    block = jnp.zeros((PAD, width), F32)
    for first, values in enumerate(rows):
        for index, part in enumerate(pieces(values)):
            block = jnp.where(row == 3 * first + index, part.astype(F32), block)
    return block.astype(BF16)


def unstacked(block, first):
    return jnp.sum(block.astype(F32)[3 * first : 3 * first + 3, :], axis=0, keepdims=True)


def from_sides(low_source, high_source, axis):
    count = lax.axis_size(axis)
    if count == 2:
        index = lax.axis_index(axis)
        sent = jnp.where(index == 0, low_source, high_source)
        got = lax.ppermute(sent, axis, [(0, 1), (1, 0)])
        return got, got
    forward = [(i, i + 1) for i in range(count - 1)]
    backward = [(i + 1, i) for i in range(count - 1)]
    return lax.ppermute(low_source, axis, forward), lax.ppermute(high_source, axis, backward)


def edges(block, axis):
    count = lax.axis_size(axis)
    if count == 2:
        return lax.ppermute(block, axis, [(0, 1), (1, 0)])
    low, high = from_sides(block, block, axis)
    width = block.shape[-1]
    lane = lax.broadcasted_iota(jnp.int32, block.shape, block.ndim - 1)
    return jnp.where(lane < width // 2, high, low)


def surroundings(block, before_corner=None):
    rows = block.shape[0]
    above, below = from_sides(block[rows - HALF :], block[:HALF], "rows")
    side = edges(block, "cols")
    if before_corner is not None:
        above, below = after((above, below), before_corner)
    if lax.axis_size("rows") == 2:
        corner = edges(above, "cols")
        return block, above, below, side, corner, corner
    return block, above, below, side, edges(above, "cols"), edges(below, "cols")


def flag(test):
    return jnp.where(test, 1.0, 0.0).astype(F32)


def fill_shifts(shifts):
    width = shifts.shape[0] // 2
    col = lax.axis_index("cols")
    has_right, has_left = flag(col < lax.axis_size("cols") - 1), flag(col > 0)
    source = lax.broadcasted_iota(jnp.int32, (width, width), 0)
    target = lax.broadcasted_iota(jnp.int32, (width, width), 1)
    for tap in range(KS):
        cut = slice(tap * width, (tap + 1) * width)
        wanted = target + (tap - HALF)
        shifts[:width, cut] = jnp.where(source == wanted, 1.0, 0.0).astype(BF16)
        right = jnp.where(source + width == wanted, has_right, 0.0)
        left = jnp.where(source - width == wanted, has_left, 0.0)
        shifts[width:, cut] = (right + left).astype(BF16)


def shifted_rows(refs, shifts, at, count):
    block, above, below, side, above_side, below_side = refs
    row = lax.axis_index("rows")
    has_above = flag(row > 0).astype(BF16)
    has_below = flag(row < lax.axis_size("rows") - 1).astype(BF16)
    rows = block.shape[0]
    cut = pl.ds(at, count)
    found = [jnp.concatenate([above[k, cut], above_side[k, cut]], axis=1) * has_above for k in range(HALF)]
    found += [jnp.concatenate([block[k, cut], side[k, cut]], axis=1) for k in range(rows)]
    found += [jnp.concatenate([below[k, cut], below_side[k, cut]], axis=1) * has_below for k in range(HALF)]
    return dot(jnp.concatenate(found, axis=0), shifts[...], ROWS_BY_COLS)


def convolve(refs, shifts, taps, at, count, flipped):
    rows, _, width = refs[0].shape
    moved = shifted_rows(refs, shifts, at, count)
    sums = [None] * rows
    for tap_col in range(KS):
        near = [
            moved[k * count : (k + 1) * count, tap_col * width : (tap_col + 1) * width]
            for k in range(rows + KS - 1)
        ]
        for tap_row in range(KS):
            tap = tap_row * KS + tap_col
            tap = KS * KS - 1 - tap if flipped else tap
            weight = jnp.broadcast_to(taps[:, tap : tap + 1], (count, width))
            for k in range(rows):
                term = weight * near[k + tap_row]
                sums[k] = term if sums[k] is None else sums[k] + term
    return sums


def forward_conv_kernel(block, above, below, side, above_side, below_side, kernel, packed, centered, local, shifts):
    refs = (block, above, below, side, above_side, below_side)
    rows, channels, width = block.shape
    fill_shifts(shifts)

    def step(index, totals):
        at = pl.multiple_of(index * PAD, PAD)
        sums = convolve(refs, shifts, kernel[pl.ds(at, PAD), :], at, PAD, False)
        for k in range(rows):
            centered[pl.ds(at, PAD), k * width : (k + 1) * width] = sums[k]
        return tuple(total + value[:8] + value[8:] for total, value in zip(totals, sums))

    totals = lax.fori_loop(
        0, channels // PAD, step, tuple(jnp.zeros((8, width), F32) for _ in range(rows)), unroll=2
    )
    mean = jnp.concatenate([jnp.sum(total, axis=0, keepdims=True) for total in totals], axis=1) / channels
    local[...] = jnp.broadcast_to(mean, local.shape)

    def finish(index, carry):
        at = pl.multiple_of(index * PAD, PAD)
        value = centered[pl.ds(at, PAD), :] - mean
        centered[pl.ds(at, PAD), :] = value
        packed[pl.ds(at, PAD), :] = value.astype(BF16)
        return carry

    lax.fori_loop(0, channels // PAD, finish, 0, unroll=2)
    packed[channels:, :] = stacked_rows(mean)


def shift_scratch(width):
    return [pltpu.VMEM((2 * width, KS * width), BF16)]


def forward_conv(around, kernel):
    rows, channels, width = around[0].shape
    pixels = rows * width
    return pl.pallas_call(
        forward_conv_kernel,
        out_shape=(
            shape((channels + PAD, pixels), BF16),
            shape((channels, pixels), F32),
            shape((8, pixels), F32),
        ),
        in_specs=[whole] * 7,
        out_specs=(whole,) * 3,
        scratch_shapes=shift_scratch(width),
        compiler_params=params(32),
        cost_estimate=LIGHT,
        name="conv_forward",
    )(*around, kernel)


def backward_conv_kernel(block, above, below, side, above_side, below_side, kernel, cotangent, result, shifts):
    refs = (block, above, below, side, above_side, below_side)
    rows, channels, width = block.shape
    fill_shifts(shifts)

    def step(index, carry):
        at = pl.multiple_of(index * PAD, PAD)
        sums = convolve(refs, shifts, kernel[pl.ds(at, PAD), :], at, PAD, True)
        for k in range(rows):
            result[k, pl.ds(at, PAD)] = (sums[k] + cotangent[k, pl.ds(at, PAD)].astype(F32)).astype(BF16)
        return carry

    lax.fori_loop(0, channels // PAD, step, 0, unroll=2)


def backward_conv(around, kernel, cotangent):
    return pl.pallas_call(
        backward_conv_kernel,
        out_shape=shape(cotangent.shape, BF16),
        in_specs=[whole] * 8,
        out_specs=whole,
        scratch_shapes=shift_scratch(cotangent.shape[2]),
        compiler_params=params(32),
        cost_estimate=LIGHT,
        name="conv_backward",
    )(*around, kernel, cotangent)


def kernel_gradient_kernel(block, above, below, side, above_side, below_side, gradient, result, shifts):
    refs = (block, above, below, side, above_side, below_side)
    rows, channels, width = block.shape
    fill_shifts(shifts)

    def step(index, carry):
        at = pl.multiple_of(index * PAD, PAD)
        moved = shifted_rows(refs, shifts, at, PAD)
        lane = lax.broadcasted_iota(jnp.int32, (PAD, width), 1)
        grads = [gradient[k, pl.ds(at, PAD)].astype(F32) for k in range(rows)]
        sums = jnp.zeros((PAD, width), F32)
        for tap_col in range(KS):
            near = [
                moved[k * PAD : (k + 1) * PAD, tap_col * width : (tap_col + 1) * width]
                for k in range(rows + KS - 1)
            ]
            for tap_row in range(KS):
                total = grads[0] * near[tap_row]
                for k in range(1, rows):
                    total = total + grads[k] * near[k + tap_row]
                tap = tap_row * KS + tap_col
                sums = jnp.where(lane == tap, jnp.sum(total, axis=1, keepdims=True), sums)
        result[pl.ds(at, PAD), :] = sums
        return carry

    lax.fori_loop(0, channels // PAD, step, 0, unroll=2)


def kernel_gradient(around, gradient):
    rows, channels, width = gradient.shape
    return pl.pallas_call(
        kernel_gradient_kernel,
        out_shape=shape((channels, width), F32),
        in_specs=[whole] * 7,
        out_specs=whole,
        scratch_shapes=shift_scratch(width),
        compiler_params=params(32),
        cost_estimate=LIGHT,
        name="kernel_gradient",
    )(*around, gradient)


def pack_kernel(cotangent, scale, gain, packed, gain_rows):
    rows, channels, width = cotangent.shape
    ones = jnp.ones((PAD, width), BF16)
    wide = dot(stacked_rows(scale[...].reshape(1, channels)), ones, COLS_BY_COLS)
    for k in range(rows):
        packed[:, k * width : (k + 1) * width] = (cotangent[k].astype(F32) * wide).astype(BF16)
    gain_rows[...] = stacked_rows(gain[...].reshape(1, channels))


def pack_cotangent(cotangent, scale, gain):
    rows, channels, width = cotangent.shape
    return pl.pallas_call(
        pack_kernel,
        out_shape=(shape((channels, rows * width), BF16), shape((PAD, channels), BF16)),
        in_specs=[whole] * 3,
        out_specs=(whole, whole),
        compiler_params=params(60),
        cost_estimate=LIGHT,
        name="pack_cotangent",
    )(cotangent, scale, gain)


def gelu_parts(values):
    cdf = 0.5 * (1.0 + lax.erf(values * 0.7071067811865476))
    slope = cdf + values * jnp.exp(-0.5 * values * values) * 0.3989422804014327
    return values * cdf, slope


ROWS_BY_COLS = (((1,), (0,)), ((), ()))
COLS_BY_COLS = (((0,), (0,)), ((), ()))
ROWS_BY_ROWS = (((1,), (1,)), ((), ()))


def dot(left, right, dims):
    return lax.dot_general(left, right, dims, preferred_element_type=F32)


def tile_of(hidden_units):
    for size in (256, 128):
        if hidden_units % size == 0:
            return size
    return hidden_units


def fixed(dims):
    return pl.BlockSpec(dims, lambda t: (0,) * len(dims))


def rows_of(tile, width, first=0):
    return pl.BlockSpec((tile, width), lambda t: (t + first, 0))


def columns_of(height, tile, first=0):
    return pl.BlockSpec((height, tile), lambda t: (0, t + first))


def rotated(block):
    count = lax.axis_size("chan")
    return [block] + [
        lax.ppermute(block, "chan", [(i, (i + k) % count) for i in range(count)])
        for k in range(1, count)
    ]


def cot_kernel(cot_all, w_reduce, bias, *refs):
    shares, (gain, wide_bias, back, matrix) = refs[:-4], refs[-4:]
    count, channels, _ = cot_all.shape

    @pl.when(pl.program_id(0) == 0)
    def _():
        ones = jnp.ones((PAD, gain.shape[1]), BF16)
        wide_bias[...] = dot(stacked_rows(bias[...]), ones, COLS_BY_COLS)
        unpack(cot_all, matrix)
        for k in range(count):
            if len(shares) == 1:
                place, share = k, shares[0][k]
            else:
                place, share = lax.rem(lax.axis_index("chan") + count - k, count), shares[k][...]
            at = pl.multiple_of(place * channels, PAD)
            gain[pl.ds(at, channels), :] = dot(share, ones, COLS_BY_COLS)

    back[...] = dot(w_reduce[...], matrix[...], COLS_BY_COLS)


def cot_stage(cot_all, w_reduce, bias, shares):
    pixels = cot_all.shape[2]
    every, units = w_reduce.shape
    tile = tile_of(units)
    return pl.pallas_call(
        cot_kernel,
        grid=(units // tile,),
        out_shape=(shape((every, 128), F32), shape((units, 128), F32), shape((units, pixels), F32)),
        in_specs=[fixed(cot_all.shape), columns_of(every, tile), fixed((1, units))]
        + [fixed(share.shape) for share in shares],
        out_specs=(fixed((every, 128)), fixed((units, 128)), rows_of(tile, pixels)),
        scratch_shapes=[pltpu.VMEM((every, pixels), BF16)],
        compiler_params=params(60),
        cost_estimate=LIGHT,
        name="cotangent_stage",
    )(cot_all, w_reduce, bias[None, :], *shares)


def widened(values, pixels):
    return jnp.concatenate([values] * (pixels // values.shape[1]), axis=1)


def normalise(conv_all, gain, normed):
    count, padded, pixels = conv_all.shape
    channels = padded - PAD
    every = count * channels
    means = [jnp.sum(conv_all[k, channels:, :].astype(F32), axis=0, keepdims=True) for k in range(count)]
    mean = means[0]
    for k in range(1, count):
        mean = mean + means[k]
    mean = mean / count
    squares = jnp.zeros((8, pixels), F32)
    for k in range(count):
        moved = means[k] - mean

        def gather(index, total):
            at = pl.multiple_of(index * PAD, PAD)
            value = conv_all[k, pl.ds(at, PAD), :].astype(F32) + moved
            value = value * value
            return total + value[:8] + value[8:]

        squares = lax.fori_loop(0, channels // PAD, gather, squares, unroll=2)
    deviation = lax.rsqrt(jnp.sum(squares, axis=0, keepdims=True) / every + EPSILON)
    for k in range(count):
        moved = means[k] - mean

        def write(index, carry):
            at = pl.multiple_of(index * PAD, PAD)
            to = pl.multiple_of(k * channels + at, PAD)
            value = (conv_all[k, pl.ds(at, PAD), :].astype(F32) + moved) * deviation
            scale = gain[pl.ds(to, PAD), :]
            for p in range(pixels // 128):
                cut = slice(p * 128, (p + 1) * 128)
                normed[pl.ds(to, PAD), cut] = (value[:, cut] * scale).astype(BF16)
            return carry

        lax.fori_loop(0, channels // PAD, write, 0, unroll=2)
    return mean, deviation


def norm_kernel(conv_all, gain, normed, stats):
    mean, deviation = normalise(conv_all, gain, normed)
    row = lax.broadcasted_iota(jnp.int32, stats.shape, 0)
    stats[...] = jnp.where(row == 0, mean, jnp.where(row == 1, deviation, 0.0))


def norm_stage(conv_all, gain):
    pixels = conv_all.shape[2]
    return pl.pallas_call(
        norm_kernel,
        out_shape=(shape((gain.shape[0], pixels), BF16), shape((8, pixels), F32)),
        in_specs=[whole] * 2,
        out_specs=(whole, whole),
        compiler_params=params(32),
        cost_estimate=LIGHT,
        name="norm",
    )(conv_all, gain)


def block_kernel(steps, normed, gain, w_expand, bias, back, hidden, grad_pre, *refs):
    blocks, normed_sum = refs[:-1], refs[-1]
    at = pl.program_id(0)

    @pl.when(at == 0)
    def _():
        normed_sum[...] = jnp.zeros_like(normed_sum)

    pre = dot(w_expand[...], normed[...], ROWS_BY_COLS) + widened(bias[...], normed.shape[1])
    active, slope = gelu_parts(pre)
    hidden[...] = active.astype(BF16)
    grad = (back[...] * slope).astype(BF16)
    grad_pre[...] = grad
    normed_sum[...] += dot(w_expand[...], grad, COLS_BY_COLS)

    @pl.when(at == steps - 1)
    def _():
        every, pixels = normed.shape
        def step(index, totals):
            cut = pl.ds(pl.multiple_of(index * PAD, PAD), PAD)
            value = normed_sum[cut, :]
            first = value * widened(gain[cut, :], pixels)
            cross = value * normed[cut, :].astype(F32)
            return totals[0] + first[:8] + first[8:], totals[1] + cross[:8] + cross[8:]

        totals = lax.fori_loop(0, every // PAD, step, (jnp.zeros((8, pixels), F32),) * 2, unroll=2)
        moments = stacked_rows(*[jnp.sum(total, axis=0, keepdims=True) for total in totals])
        for k, block in enumerate(blocks):
            height = block.shape[0] - PAD
            place = lax.rem(lax.axis_index("chan") + k, len(blocks)) if len(blocks) > 1 else 0
            block[:height, :] = normed_sum[pl.ds(pl.multiple_of(place * height, PAD), height), :].astype(BF16)
            block[height:, :] = moments


def block_stage(normed, gain, w_expand, bias, back):
    count = lax.axis_size("chan")
    units, every = w_expand.shape
    pixels = normed.shape[1]
    tile = 512 if units % 512 == 0 else tile_of(units)
    steps = units // tile
    blocks = count if count <= 4 else 1
    return pl.pallas_call(
        functools.partial(block_kernel, steps),
        grid=(steps,),
        out_shape=(shape((units, pixels), BF16),) * 2
        + (shape((every // blocks + PAD, pixels), BF16),) * blocks,
        in_specs=[
            fixed(normed.shape),
            fixed(gain.shape),
            rows_of(tile, every),
            rows_of(tile, 128),
            rows_of(tile, pixels),
        ],
        out_specs=(rows_of(tile, pixels),) * 2 + (fixed((every // blocks + PAD, pixels)),) * blocks,
        scratch_shapes=[pltpu.VMEM((every, pixels), F32)],
        compiler_params=params(60),
        cost_estimate=LIGHT,
        name="pointwise_block",
    )(normed, gain, w_expand, bias, back)


def reduced_kernel(weight, hidden, result):
    result[...] = dot(weight[...], hidden[...], ROWS_BY_COLS).astype(BF16)


def reduce_product(w_reduce, hidden):
    every, units = w_reduce.shape
    pixels = hidden.shape[1]
    tile = 512 if every % 512 == 0 else tile_of(every)
    return pl.pallas_call(
        reduced_kernel,
        grid=(every // tile,),
        out_shape=shape((every, pixels), BF16),
        in_specs=[rows_of(tile, units), fixed(hidden.shape)],
        out_specs=rows_of(tile, pixels),
        compiler_params=params(60),
        cost_estimate=LIGHT,
        name="reduced_product",
    )(w_reduce, hidden)


def unpack(cot_all, target):
    channels = cot_all.shape[1]
    for k in range(cot_all.shape[0]):
        target[k * channels : (k + 1) * channels, :] = cot_all[k]


def own_tile_kernel(normed, cot_all, hidden, grad_pre, grad_reduce, grad_expand, cot):
    @pl.when(pl.program_id(0) == 0)
    def _():
        unpack(cot_all, cot)

    grad_reduce[...] = dot(cot[...], hidden[...], ROWS_BY_ROWS).astype(BF16)
    grad_expand[...] = dot(grad_pre[...], normed[...], ROWS_BY_ROWS).astype(BF16)


def own_tile_gradients(normed, cot_all, hidden, grad_pre):
    every, pixels = normed.shape
    units = hidden.shape[0]
    tile = 512 if units % 512 == 0 else tile_of(units)
    return pl.pallas_call(
        own_tile_kernel,
        grid=(units // tile,),
        out_shape=(shape((every, units), BF16), shape((units, every), BF16)),
        in_specs=[fixed(normed.shape), fixed(cot_all.shape), rows_of(tile, pixels), rows_of(tile, pixels)],
        out_specs=(columns_of(every, tile), rows_of(tile, every)),
        scratch_shapes=[pltpu.VMEM((every, pixels), BF16)],
        compiler_params=params(60),
        cost_estimate=LIGHT,
        name="own_tile_gradients",
    )(normed, cot_all, hidden, grad_pre)


def plus(first, product):
    return (first.astype(F32) + product.astype(BF16).astype(F32)).astype(BF16)


def other_tile_kernel(
    normed, cot_all, reduce_own, expand_own, w_expand, bias, w_reduce, grad_reduce, grad_expand, cot
):
    @pl.when(pl.program_id(0) == 0)
    def _():
        unpack(cot_all, cot)

    pre = dot(w_expand[...], normed[...], ROWS_BY_COLS) + widened(bias[...], normed.shape[1])
    back = dot(w_reduce[...], cot[...], COLS_BY_COLS)
    active, slope = gelu_parts(pre)
    grad_pre = (back * slope).astype(BF16)
    grad_reduce[...] = plus(reduce_own[...], dot(cot[...], active.astype(BF16), ROWS_BY_ROWS))
    grad_expand[...] = plus(expand_own[...], dot(grad_pre, normed[...], ROWS_BY_ROWS))


def two_tile_gradients(normed, cot_all, reduce_own, expand_own, w_expand, bias, w_reduce):
    every, pixels = normed.shape
    units = w_expand.shape[0]
    tile = 384 if units % 384 == 0 else tile_of(units)
    return pl.pallas_call(
        other_tile_kernel,
        grid=(units // tile,),
        out_shape=(shape((every, units), BF16), shape((units, every), BF16)),
        in_specs=[
            fixed(normed.shape),
            fixed(cot_all.shape),
            columns_of(every, tile),
            rows_of(tile, every),
            rows_of(tile, every),
            rows_of(tile, 128),
            columns_of(every, tile),
        ],
        out_specs=(columns_of(every, tile), rows_of(tile, every)),
        scratch_shapes=[pltpu.VMEM((every, pixels), BF16)],
        compiler_params=params(60),
        cost_estimate=LIGHT,
        name="two_tile_gradients",
    )(normed, cot_all, reduce_own, expand_own, w_expand, bias, w_reduce)


def pair_sum(mine, theirs):
    return (mine.astype(F32) + theirs.astype(F32)).astype(BF16)


def norm_gradient_kernel(every, centered, local, stats, gain, *refs):
    blocks, result = refs[:-1], refs[-1]
    rows, channels, width = result.shape
    mean, deviation = stats[0:1, :], stats[1:2, :]
    first = cross = 0.0
    for block in blocks:
        tail = block[channels:, :]
        first = first + unstacked(tail, 0)
        cross = cross + unstacked(tail, 1)
    first, cross = first / every, cross / every
    shift = local[0:1, :] - mean
    own = lax.axis_index("chan") * channels

    def step(index, carry):
        at = pl.multiple_of(index * PAD, PAD)
        cut = pl.ds(at, PAD)
        hat = (centered[cut, :] + shift) * deviation
        value = blocks[0][cut, :].astype(F32)
        for block in blocks[1:]:
            value = value + block[cut, :].astype(F32)
        value = value * widened(gain[pl.ds(pl.multiple_of(own + at, PAD), PAD), :], value.shape[1])
        value = ((value - first - hat * cross) * deviation).astype(BF16)
        for k in range(rows):
            result[k, cut] = value[:, k * width : (k + 1) * width]
        return carry

    lax.fori_loop(0, channels // PAD, step, 0)


def norm_gradient(every, dims, blocks, centered, local, stats, gain):
    return pl.pallas_call(
        functools.partial(norm_gradient_kernel, every),
        out_shape=shape(dims, BF16),
        in_specs=[whole] * (4 + len(blocks)),
        out_specs=whole,
        compiler_params=params(32),
        cost_estimate=LIGHT,
        name="norm_gradient",
    )(centered, local, stats, gain, *blocks)


def scattered(blocks):
    count = lax.axis_size("chan")
    if len(blocks) == 1:
        height = blocks[0].shape[0] - PAD
        total = lax.psum_scatter(blocks[0][:height], "chan", scatter_dimension=0, tiled=True)
        tail = blocks[0][height:].astype(F32)
        sums = jnp.stack([jnp.sum(tail[:3], axis=0), jnp.sum(tail[3:6], axis=0)])
        sums = lax.psum(sums, "chan")
        parts = [part for row in sums for part in pieces(row)]
        tail = jnp.zeros(tail.shape, BF16).at[:6].set(jnp.stack(parts))
        return [jnp.concatenate([total, tail])]
    return [blocks[0]] + [
        lax.ppermute(blocks[k], "chan", [(i, (i + k) % count) for i in range(count)])
        for k in range(1, count)
    ]


def after(values, *others):
    return lax.optimization_barrier((values, others))[0]


def swap(values, axis):
    return lax.ppermute(values, axis, [(0, 1), (1, 0)])


def on_device(
    image, kernel, layer_norm_weight, w_expand, bias_expand, w_reduce, layer_scale, cotangent
):
    channels, tile_rows, tile_cols = image.shape
    pixels = tile_rows * tile_cols
    every = w_reduce.shape[0]
    two_tiles = lax.axis_size("rows") == 2 and lax.axis_size("cols") == 2

    image_rows = jnp.transpose(image, (1, 0, 2))
    around = surroundings(image_rows)
    cot_rows = jnp.transpose(cotangent, (1, 0, 2))
    packed_cot, gain_rows = pack_cotangent(cot_rows, layer_scale, layer_norm_weight)
    cot_all = lax.all_gather(packed_cot, "chan")

    packed_conv, centered, local = forward_conv(around, kernel)
    conv_all = lax.all_gather(packed_conv, "chan")
    cot_all, bias = after((cot_all, bias_expand), packed_conv)
    gain_rows = after(gain_rows, packed_conv)
    count = lax.axis_size("chan")
    shares = [lax.all_gather(gain_rows, "chan")]
    if count <= 4:
        turns = [[(i, (i + k) % count) for i in range(count)] for k in range(1, count)]
        shares = [gain_rows] + [lax.ppermute(gain_rows, "chan", turn) for turn in turns]
    gain, bias, back = cot_stage(cot_all, w_reduce, bias, shares)
    normed, stats = norm_stage(conv_all, gain)
    ready = normed
    if two_tiles:
        cot_other = swap(cot_all, "rows")
        normed_other = swap(normed, "rows")
        ready = after(normed, cot_other)
    hidden, grad_pre, *blocks = block_stage(ready, gain, w_expand, bias, back)
    norm_inputs = (scattered(blocks), centered, local, stats)
    product = reduce_product(w_reduce, hidden)
    reduced = lax.psum_scatter(product, "chan", scatter_dimension=0, tiled=True)

    if two_tiles:
        own = own_tile_gradients(normed, cot_all, after(hidden, product), grad_pre)
        found = two_tile_gradients(normed_other, cot_other, *own, w_expand, bias, w_reduce)
        norm_inputs = after(norm_inputs, found)
    gradient = norm_gradient(every, image_rows.shape, *norm_inputs, gain)
    taps = kernel_gradient(around, gradient)
    grad_around = surroundings(gradient, taps if two_tiles else None)
    if two_tiles:
        theirs = [swap(after(mine, gradient), "cols") for mine in found]
        grad_reduce = pair_sum(found[0], theirs[0])
        grad_around = after(grad_around, grad_reduce)
    grad_rows = backward_conv(grad_around, kernel, cot_rows)
    grad_input = jnp.transpose(grad_rows, (1, 0, 2))
    if two_tiles:
        taps = after(taps, grad_rows)
        taps = taps + swap(taps, "cols")
        taps = taps + swap(taps, "rows")
        grad_expand = pair_sum(found[1], theirs[1])
        reduced = after(reduced, grad_expand, taps)
    else:
        taps = lax.psum(taps, ("rows", "cols"))
        cot = cot_all[:, :channels, :].reshape(every, pixels)
        grad_reduce = dot(cot, hidden, ROWS_BY_ROWS).astype(BF16)
        grad_expand = dot(grad_pre, normed, ROWS_BY_ROWS).astype(BF16)
        grad_reduce, grad_expand = lax.psum((grad_reduce, grad_expand), ("rows", "cols"))
    taps = taps[:, : KS * KS]

    output = (
        image.reshape(channels, pixels).astype(F32) + layer_scale[:, None] * reduced.astype(F32)
    ).astype(BF16).reshape(image.shape)
    return output, grad_input, grad_expand, grad_reduce, taps


def solution(mesh):
    placed = (
        P("chan", ("groups", "rows"), "cols"),
        P("chan", None),
        P("chan"),
        P("chan", None),
        P("chan"),
        P(None, "chan"),
        P("chan"),
        P("chan", ("groups", "rows"), "cols"),
    )
    return jax.shard_map(
        on_device,
        mesh=mesh,
        in_specs=placed,
        out_specs=(
            P("chan", ("groups", "rows"), "cols"),
            P("chan", ("groups", "rows"), "cols"),
            P(("groups", "chan"), None),
            P("groups", "chan"),
            P(("groups", "chan"), None),
        ),
        check_vma=False,
    )
```
